256 devices in a mesh: dp: 16 (over x_lo, y, core), ctx: 16 (over x_hi, z).
Axes of the slice: x: 4 (x_hi: 2, x_lo: 2; x = x_hi * 2 + x_lo), y: 4, z: 8, core: 2. Of those that a mesh axis runs over, the one named last changes fastest.
Arguments:
- query_rows: bfloat16 [65536, 1024], P(('dp', 'ctx')), parts along dimension 0, may hold values from -8 to 8
- key_rows: bfloat16 [65536, 128], P(('dp', 'ctx')), parts along dimension 0, may hold values from -8 to 8
- value_rows: bfloat16 [65536, 128], P(('dp', 'ctx')), parts along dimension 0, may hold values from -6 to 6
- out_grad: bfloat16 [65536, 1024], P(('dp', 'ctx')), parts along dimension 0, may hold values from -6 to 6
- doc_lengths: int32 [256], P('dp'), parts along dimension 0, may hold values from 1 to 1024, as said below
Outputs:
- query_grad: bfloat16 [65536, 1024], P(('dp', 'ctx')), parts along dimension 0
- key_grad: bfloat16 [65536, 128], P(('dp', 'ctx')), parts along dimension 0
- value_grad: bfloat16 [65536, 128], P(('dp', 'ctx')), parts along dimension 0
The draws below stay inside these ranges and needn't reach their ends.
There are 16 independent parts, one for each index of `dp`. The reference program is written for one: setup_inputs(seed, part) draws one part's arguments, and reference() takes and returns one part's arrays. A program takes and returns all parts, laid end to end along the dimension named above; each array names one. Nothing has to cross between parts.
Inputs may be any that keep to these rules, and one draw needn't show every extreme that they name: `doc_lengths`: the lengths sum to 4096, and the first of them is exactly 1024.
All inputs are finite; a program needn't handle non-finite values.
Results may differ from the reference program's by a relative error of at most 0.0071.
Values may be sent and summed in bfloat16 or wider, within the bound.
A program may use at most 64 MiB of HBM per device.

```python
import math
import jax
import jax.numpy as jnp
from jax import lax

H = 8
DH = 128
TOK_DEV = 256
DOCS = 16
TOKENS = 4096
MOST = 1024


def draw_query_rows(key, part):
    key = jax.random.fold_in(key, 11)
    sample = jax.random.truncated_normal(key, -8.0, 8.0, (TOKENS, H * DH), jnp.float32)
    return sample.astype(jnp.bfloat16)


def draw_key_rows(key, part):
    key = jax.random.fold_in(key, 23)
    sample = jax.random.truncated_normal(key, -8.0, 8.0, (TOKENS, DH), jnp.float32)
    return sample.astype(jnp.bfloat16)


def draw_doc_lengths(key, part):
    key = jax.random.fold_in(key, 37)
    first, second, third = jax.random.split(key, 3)
    tail_length = jax.random.randint(third, (), TOK_DEV // 4, 3 * TOK_DEV // 4 + 1, dtype=jnp.int32)
    others = DOCS - 3
    remaining = TOKENS - 2 * MOST - tail_length
    base_length = remaining // others
    leftover = remaining % others
    lengths = base_length + (jnp.arange(others, dtype=jnp.int32) < leftover).astype(jnp.int32)
    pair_count = others // 2
    moved = jax.random.randint(first, (pair_count,), 0, base_length, dtype=jnp.int32)
    paired = jnp.stack([moved, -moved], axis=1).reshape(2 * pair_count)
    spread = jnp.concatenate([paired, jnp.zeros((others - 2 * pair_count,), jnp.int32)])
    lengths = lengths + spread
    order = jax.random.permutation(second, others)
    lengths = lengths[order]
    head = jnp.full((1,), MOST, jnp.int32)
    return jnp.concatenate([head, lengths, head, tail_length[None]]).astype(jnp.int32)


def block_levels(rng, dims, shards, least, high):
    loudness, own = 1.0, jax.random.fold_in(rng, 6)
    for dim, blocks in shards:
        draws = jnp.exp(jax.random.uniform(jax.random.fold_in(own, dim), (blocks,), jnp.float32, least / len(shards), high / len(shards)))
        loudness = loudness * jnp.repeat(draws, dims[dim] // blocks).reshape([-1 if axis == dim else 1 for axis in range(len(dims))])
    return loudness


def gaussian(own_key, extent, scale, reach, pieces=(), kind=jnp.bfloat16):
    loudness = block_levels(own_key, extent, pieces, -0.22, 0.18) if pieces else 1.0
    result = jax.random.normal(own_key, extent, jnp.float32) * scale * loudness
    return jnp.minimum(jnp.maximum(result, -reach), reach).astype(kind)


def setup_inputs(seed: int = 0, part: int = 0) -> dict:
    key_list = jax.random.split(jax.random.key(seed), 6)
    part_splits = jax.random.split(jax.random.fold_in(key_list[5], part), 6)
    return {
        "query_rows": draw_query_rows(jax.random.fold_in(jax.random.fold_in(key_list[5], part), 71), part),
        "key_rows": draw_key_rows(jax.random.fold_in(jax.random.fold_in(key_list[5], part), 71), part),
        "value_rows": gaussian(part_splits[2], (TOKENS, DH), 1.0, 6.0, ((0, 16),)),
        "out_grad": gaussian(part_splits[3], (TOKENS, H * DH), 1.0, 6.0, ((0, 16),)),
        "doc_lengths": draw_doc_lengths(jax.random.fold_in(jax.random.fold_in(key_list[5], part), 71), part),
    }


masked_value = -1e+30

def doc_numbers(positions, doc_ends):
    return lax.optimization_barrier(jnp.sum((positions[:, None] >= doc_ends[None, :]).astype(jnp.int32), axis=1))

def reference(query_rows, key_rows, value_rows, out_grad, doc_lengths):
    score_scale = 1.0 / math.sqrt(DH)
    doc_ends = jnp.cumsum(doc_lengths).astype(jnp.int32)
    positions = jnp.arange(TOKENS, dtype=jnp.int32)
    documents = doc_numbers(positions, doc_ends)
    block_rows = min(512, TOKENS)
    block_count = TOKENS // block_rows
    keys_wide = key_rows.astype(jnp.float32)
    values_wide = value_rows.astype(jnp.float32)
    query_blocks = query_rows.reshape(block_count, block_rows, H, DH)
    grad_blocks = out_grad.reshape(block_count, block_rows, H, DH)
    doc_blocks = documents.reshape(block_count, block_rows)
    place_blocks = positions.reshape(block_count, block_rows)

    def one_block(carry, inputs):
        key_acc, value_acc = carry
        queries, grads_out, query_docs, query_places = inputs
        queries_wide = queries.astype(jnp.float32)
        grads_wide = grads_out.astype(jnp.float32)
        allowed = ((query_docs[:, None] == documents[None, :]) & (positions[None, :] <= query_places[:, None]))[:, None, :]
        raw_scores = jnp.einsum('thd,sd->ths', queries_wide, keys_wide) * score_scale
        masked = jnp.where(allowed, raw_scores, masked_value)
        grad_dots = jnp.einsum('thd,sd->ths', grads_wide, values_wide)
        row_top = lax.optimization_barrier(jnp.max(masked, axis=2))
        row_total = lax.optimization_barrier(jnp.sum(jnp.exp(masked - row_top[:, :, None]), axis=2))
        log_total = row_top + jnp.log(row_total)
        softmax = jnp.exp(masked - log_total[:, :, None])
        row_delta = lax.optimization_barrier(jnp.sum(softmax * grad_dots, axis=2))
        score_grad = softmax * (grad_dots - row_delta[:, :, None])
        soft_low = lax.optimization_barrier(softmax.astype(jnp.bfloat16)).astype(jnp.float32)
        grad_low = lax.optimization_barrier(score_grad.astype(jnp.bfloat16)).astype(jnp.float32)
        value_acc = value_acc + jnp.einsum('ths,thd->sd', soft_low, grads_wide)
        key_acc = key_acc + jnp.einsum('ths,thd->sd', grad_low, queries_wide) * score_scale
        query_part = jnp.einsum('ths,sd->thd', grad_low, keys_wide) * score_scale
        return ((key_acc, value_acc), query_part.reshape(block_rows, H * DH).astype(jnp.bfloat16))
    zeros_kv = jnp.zeros((TOKENS, DH), jnp.float32)
    (key_acc, value_acc), query_parts = lax.scan(one_block, (zeros_kv, zeros_kv), (query_blocks, grad_blocks, doc_blocks, place_blocks))
    query_grad = query_parts.reshape(TOKENS, H * DH)
    return (query_grad, key_acc.astype(jnp.bfloat16), value_acc.astype(jnp.bfloat16))
```

```python
import functools
import math

import jax
import jax.numpy as jnp
from jax import lax
from jax.experimental import pallas as pl
from jax.experimental.pallas import tpu as pltpu
from jax.sharding import PartitionSpec as P

MESH = pl.DeviceIdType.MESH
MASKED = -1e30
HEADS = 8
WIDTH = 128
ROWS = 256
REACH = 4
FIRST = 4
DOCS = 16


def attention_kernel(
    size,
    lengths,
    q_hbm,
    k_hbm,
    v_hbm,
    o_hbm,
    dq_out,
    dk_out,
    dv_out,
    q_ref,
    o_ref,
    keys,
    values,
    keys_turned,
    bias,
    weights,
    dots,
    tops,
    totals,
    weighted,
    factors,
    deltas,
    dq_acc,
    key_part,
    value_part,
    send_box,
    recv_box,
    load_sem,
    kv_send_sem,
    kv_recv_sem,
    grad_send_sem,
    grad_recv_sem,
):
    me = lax.axis_index("ctx")
    depth = jnp.where(me < FIRST, me, me - FIRST)
    has_left = depth > 0
    has_right = (me != FIRST - 1) & (me != size - 1)
    left = jnp.maximum(me - 1, 0)
    right = jnp.minimum(me + 1, size - 1)

    loads = [
        pltpu.make_async_copy(k_hbm, keys.at[0], load_sem.at[0]),
        pltpu.make_async_copy(v_hbm, values.at[0], load_sem.at[1]),
        pltpu.make_async_copy(q_hbm, q_ref, load_sem.at[2]),
        pltpu.make_async_copy(o_hbm, o_ref, load_sem.at[3]),
    ]
    for load in loads:
        load.start()

    barrier = pltpu.get_barrier_semaphore()

    @pl.when(has_left)
    def _():
        pl.semaphore_signal(barrier, inc=1, device_id={"ctx": left}, device_id_type=MESH)

    @pl.when(has_right)
    def _():
        pl.semaphore_signal(barrier, inc=1, device_id={"ctx": right}, device_id_type=MESH)

    pl.semaphore_wait(barrier, has_left.astype(jnp.int32) + has_right.astype(jnp.int32))

    def forward(k, part):
        place = (keys, values)[part]
        source = (k_hbm, v_hbm)[part] if k == 0 else place.at[k]
        return pltpu.make_async_remote_copy(
            src_ref=source,
            dst_ref=place.at[k + 1],
            send_sem=kv_send_sem.at[k, part],
            recv_sem=kv_recv_sem.at[k + 1, part],
            device_id={"ctx": right},
            device_id_type=MESH,
        )

    def send_forward(k, part):
        @pl.when(has_right & (depth >= k))
        def _():
            forward(k, part).start()

    send_forward(0, 0)
    send_forward(0, 1)

    places = me * ROWS + lax.broadcasted_iota(jnp.int32, (8, ROWS), 1)
    starts = jnp.zeros((8, ROWS), jnp.int32)
    end = jnp.int32(0)
    for d in range(DOCS):
        end = end + lengths[d]
        starts = jnp.where(places >= end, end, starts)
    places, starts = places[:1], starts[:1]

    def make_bias(k):
        key_places = (me - k) * ROWS + lax.broadcasted_iota(jnp.int32, (ROWS, ROWS), 0)
        allowed = (key_places >= starts) & (key_places <= places)
        bias[k] = jnp.where(allowed, 0.0, MASKED)

    to_log2 = math.log2(math.e) / math.sqrt(WIDTH)
    score_scale = 1.0 / math.sqrt(WIDTH)
    tops[...] = jnp.full(tops.shape, MASKED, jnp.float32)
    totals[...] = jnp.zeros(totals.shape, jnp.float32)
    weighted[...] = jnp.zeros(weighted.shape, jnp.float32)
    for k in range(REACH + 1):
        make_bias(k)

    def head(ref, h):
        return ref[:, h * WIDTH : (h + 1) * WIDTH]

    def scores(k):
        block = keys[k]
        for h in range(HEADS):
            raw = lax.dot_general(
                block, head(q_ref, h), (((1,), (1,)), ((), ())), preferred_element_type=jnp.float32
            )
            raw = raw * to_log2 + bias[k]
            top = jnp.max(raw, axis=0, keepdims=True)
            grown = jnp.exp2(raw - top)
            tops[k, h : h + 1, :] = top
            totals[k, h : h + 1, :] = jnp.sum(grown, axis=0, keepdims=True)
            weights[k, h] = grown
        keys_turned[k] = block.T

    def grad_dots(k):
        block = values[k]
        for h in range(HEADS):
            dot = lax.dot_general(
                block, head(o_ref, h), (((1,), (1,)), ((), ())), preferred_element_type=jnp.float32
            )
            dots[k, h] = dot
            weighted[k, h : h + 1, :] = jnp.sum(weights[k, h] * dot, axis=0, keepdims=True)

    loads[0].wait()
    loads[2].wait()
    scores(0)
    loads[1].wait()
    loads[3].wait()
    grad_dots(0)

    for k in range(1, REACH + 1):

        @pl.when(depth >= k)
        def _(k=k):
            forward(k - 1, 0).wait_recv()
            if k < REACH:
                send_forward(k, 0)
            scores(k)
            forward(k - 1, 1).wait_recv()
            if k < REACH:
                send_forward(k, 1)
            grad_dots(k)

    top = tops[0]
    for k in range(1, REACH + 1):
        top = jnp.maximum(top, tops[k])
    total = jnp.zeros_like(top)
    weight = jnp.zeros_like(top)
    for k in range(REACH + 1):
        factor = jnp.exp2(tops[k] - top)
        factors[k] = factor
        total = total + factor * totals[k]
        weight = weight + factor * weighted[k]
    inverse = 1.0 / total
    deltas[...] = weight * inverse
    for k in range(REACH + 1):
        factors[k] = factors[k] * inverse
    dq_acc[...] = jnp.zeros(dq_acc.shape, jnp.float32)

    def send_back(k, part):
        return pltpu.make_async_remote_copy(
            src_ref=send_box.at[k, part],
            dst_ref=recv_box.at[k - 1, part],
            send_sem=grad_send_sem.at[k, part],
            recv_sem=grad_recv_sem.at[k - 1, part],
            device_id={"ctx": left},
            device_id_type=MESH,
        )

    def gradients(k):
        key_sum = jnp.zeros((ROWS, WIDTH), jnp.float32)
        value_sum = jnp.zeros((ROWS, WIDTH), jnp.float32)
        for h in range(HEADS):
            soft = weights[k, h] * factors[k, h : h + 1, :]
            score_grad = soft * (dots[k, h] - deltas[h : h + 1, :])
            soft_low = soft.astype(jnp.bfloat16)
            grad_low = score_grad.astype(jnp.bfloat16)
            value_sum = value_sum + jnp.dot(soft_low, head(o_ref, h), preferred_element_type=jnp.float32)
            key_sum = key_sum + jnp.dot(grad_low, head(q_ref, h), preferred_element_type=jnp.float32)
            dq_acc[h] += jnp.dot(keys_turned[k], grad_low, preferred_element_type=jnp.float32)
        value_part[...] = value_sum
        key_part[...] = key_sum

    for k in range(REACH, -1, -1):

        @pl.when(depth >= k)
        def _(k=k):
            gradients(k)
            for part, own in ((0, value_part), (1, key_part)):
                if k < REACH:

                    @pl.when(has_right)
                    def _():
                        send_back(k + 1, part).wait_recv()
                        own[...] += recv_box[k, part].astype(jnp.float32)

                if k > 0:
                    send_box[k, part] = own[...].astype(jnp.bfloat16)
                    send_back(k, part).start()
                elif part == 0:
                    dv_out[...] = own[...].astype(jnp.bfloat16)
                else:
                    dk_out[...] = (own[...] * score_scale).astype(jnp.bfloat16)

    for h in range(HEADS):
        dq_out[:, h * WIDTH : (h + 1) * WIDTH] = (dq_acc[h] * score_scale).T.astype(jnp.bfloat16)

    for k in range(REACH):

        @pl.when(has_right & (depth >= k))
        def _(k=k):
            forward(k, 0).wait_send()
            forward(k, 1).wait_send()

    for k in range(1, REACH + 1):

        @pl.when(depth >= k)
        def _(k=k):
            send_back(k, 0).wait_send()
            send_back(k, 1).wait_send()


def shards(size, query_rows, key_rows, value_rows, out_grad, doc_lengths):
    bf16, f32 = jnp.bfloat16, jnp.float32
    blocks = REACH + 1
    in_place = pl.BlockSpec(memory_space=pl.ANY)
    in_vmem = pl.BlockSpec(memory_space=pltpu.VMEM)
    return pl.pallas_call(
        functools.partial(attention_kernel, size),
        out_shape=(
            jax.ShapeDtypeStruct(query_rows.shape, bf16),
            jax.ShapeDtypeStruct(key_rows.shape, bf16),
            jax.ShapeDtypeStruct(value_rows.shape, bf16),
        ),
        in_specs=[pl.BlockSpec(memory_space=pltpu.SMEM)] + [in_place] * 4,
        out_specs=(in_vmem, in_vmem, in_vmem),
        scratch_shapes=[
            pltpu.VMEM((ROWS, HEADS * WIDTH), bf16),
            pltpu.VMEM((ROWS, HEADS * WIDTH), bf16),
            pltpu.VMEM((blocks, ROWS, WIDTH), bf16),
            pltpu.VMEM((blocks, ROWS, WIDTH), bf16),
            pltpu.VMEM((blocks, WIDTH, ROWS), bf16),
            pltpu.VMEM((blocks, ROWS, ROWS), f32),
            pltpu.VMEM((blocks, HEADS, ROWS, ROWS), f32),
            pltpu.VMEM((blocks, HEADS, ROWS, ROWS), f32),
            pltpu.VMEM((blocks, HEADS, ROWS), f32),
            pltpu.VMEM((blocks, HEADS, ROWS), f32),
            pltpu.VMEM((blocks, HEADS, ROWS), f32),
            pltpu.VMEM((blocks, HEADS, ROWS), f32),
            pltpu.VMEM((HEADS, ROWS), f32),
            pltpu.VMEM((HEADS, WIDTH, ROWS), f32),
            pltpu.VMEM((ROWS, WIDTH), f32),
            pltpu.VMEM((ROWS, WIDTH), f32),
            pltpu.VMEM((blocks, 2, ROWS, WIDTH), bf16),
            pltpu.VMEM((blocks, 2, ROWS, WIDTH), bf16),
            pltpu.SemaphoreType.DMA((4,)),
            pltpu.SemaphoreType.DMA((blocks, 2)),
            pltpu.SemaphoreType.DMA((blocks, 2)),
            pltpu.SemaphoreType.DMA((blocks, 2)),
            pltpu.SemaphoreType.DMA((blocks, 2)),
        ],
        compiler_params=pltpu.CompilerParams(
            collective_id=0, has_side_effects=True, vmem_limit_bytes=48 * 1024 * 1024
        ),
    )(doc_lengths, query_rows, key_rows, value_rows, out_grad)


def solution(mesh):
    rows = P(("dp", "ctx"), None)
    return jax.shard_map(
        functools.partial(shards, mesh.shape["ctx"]),
        mesh=mesh,
        in_specs=(rows, rows, rows, rows, P("dp")),
        out_specs=(rows, rows, rows),
        check_vma=False,
    )
```

```python
import functools
import math

import jax
import jax.numpy as jnp
from jax import lax
from jax.experimental import pallas as pl
from jax.experimental.pallas import tpu as pltpu
from jax.sharding import PartitionSpec as P

MESH = pl.DeviceIdType.MESH
MASKED = -1e30
HEADS = 8
WIDTH = 128
ROWS = 256
HALF = ROWS // 2
REACH = 4
FIRST = 4
DOCS = 16
CHUNKS = 4


def attention_kernel(
    lengths_hbm,
    q_hbm,
    k_hbm,
    v_hbm,
    o_hbm,
    dq_out,
    dk_out,
    dv_out,
    lengths,
    q_ref,
    o_ref,
    keys,
    values,
    passing,
    keys_turned,
    bias,
    weights,
    dots,
    tops,
    totals,
    weighted,
    factors,
    deltas,
    dq_acc,
    key_part,
    value_part,
    send_box,
    recv_box,
    far_box,
    passing_back,
    load_sem,
    kv_send_sem,
    kv_recv_sem,
    grad_send_sem,
    grad_recv_sem,
    far_send_sem,
    far_recv_sem,
):
    me = lax.axis_index("ctx")
    size = 16
    depth = jnp.where(me < FIRST, me, me - FIRST)
    has_left = depth > 0
    has_right = (me != FIRST - 1) & (me != size - 1)
    left = jnp.maximum(me - 1, 0)
    right = jnp.minimum(me + 1, size - 1)

    out_far = (me >= 4) & (me < 12)
    out_relay = jnp.where(me < 6, me - 2, jnp.where(me < 10, me + 6, me - 10))
    is_relay = (me < 4) | (me >= 12)
    relay_from = jnp.where(me < 2, me + 10, jnp.where(me < 4, me + 2, me - 6))
    relay_to = jnp.where(me < 2, me + 14, jnp.where(me < 4, me + 6, me - 2))
    in_far = me >= 8
    in_relay = jnp.where(me < 10, me - 6, jnp.where(me < 14, me + 2, me - 14))
    back_far = me >= 8
    back_relay = jnp.where(me < 14, me - 6, me - 14)
    is_back_relay = me < 8
    back_relay_from = jnp.where(me < 2, me + 14, me + 6)
    back_relay_to = jnp.where(me < 2, me + 10, me + 2)
    in_back = (me >= 4) & (me < 12)
    in_back_relay = jnp.where(me < 10, me - 2, me - 10)

    loads = [
        pltpu.make_async_copy(lengths_hbm, lengths, load_sem.at[4]),
        pltpu.make_async_copy(k_hbm, keys.at[0], load_sem.at[0]),
        pltpu.make_async_copy(v_hbm, values.at[0], load_sem.at[1]),
        pltpu.make_async_copy(q_hbm, q_ref, load_sem.at[2]),
        pltpu.make_async_copy(o_hbm, o_ref, load_sem.at[3]),
    ]
    for load in loads:
        load.start()

    barrier = pltpu.get_barrier_semaphore()

    def greet(condition, device):
        @pl.when(condition)
        def _():
            pl.semaphore_signal(barrier, inc=1, device_id={"ctx": device}, device_id_type=MESH)

    greet(has_left, left)
    greet(has_right, right)
    greet(is_relay, relay_from)
    greet(in_far, in_relay)
    greet(is_back_relay, back_relay_from)
    greet(in_back, in_back_relay)
    targets = (has_left, has_right, out_far, is_relay, back_far, is_back_relay)
    pl.semaphore_wait(barrier, sum(target.astype(jnp.int32) for target in targets))

    def remote(source, target, send, recv, device):
        return pltpu.make_async_remote_copy(
            src_ref=source, dst_ref=target, send_sem=send, recv_sem=recv, device_id={"ctx": device}, device_id_type=MESH
        )

    def piece(c):
        return c // 2, pl.ds((c % 2) * HALF, HALF)

    def own_piece(c):
        part, rows = piece(c)
        return (k_hbm, v_hbm)[part].at[rows]

    def forward(k, c):
        part, rows = piece(c)
        place = (keys, values)[part]
        source = own_piece(c) if k == 0 else place.at[k, rows]
        return remote(source, place.at[k + 1, rows], kv_send_sem.at[k, c], kv_recv_sem.at[k + 1, c], right)

    def to_relay(c):
        part, rows = piece(c)
        return remote(own_piece(c), passing.at[part, rows], far_send_sem.at[0, c], far_recv_sem.at[0, c], out_relay)

    def from_relay(c):
        part, rows = piece(c)
        target = (keys, values)[part].at[REACH, rows]
        return remote(passing.at[part, rows], target, far_send_sem.at[1, c], far_recv_sem.at[1, c], relay_to)

    def send_forward(k, c):
        @pl.when(has_right & (depth >= k))
        def _():
            forward(k, c).start()

    def relay(c):
        @pl.when(is_relay)
        def _():
            to_relay(c).wait_recv()
            from_relay(c).start()

    for c in range(CHUNKS):
        send_forward(0, c)

        @pl.when(out_far)
        def _(c=c):
            to_relay(c).start()

    loads[0].wait()
    places = me * ROWS + lax.broadcasted_iota(jnp.int32, (8, ROWS), 1)
    starts = jnp.zeros((8, ROWS), jnp.int32)
    end = jnp.int32(0)
    for d in range(DOCS):
        end = end + lengths[d]
        starts = jnp.where(places >= end, end, starts)
    places, starts = places[:1], starts[:1]
    for k in range(REACH + 1):
        key_places = (me - k) * ROWS + lax.broadcasted_iota(jnp.int32, (ROWS, ROWS), 0)
        allowed = (key_places >= starts) & (key_places <= places)
        bias[k] = jnp.where(allowed, 0.0, MASKED)

    to_log2 = math.log2(math.e) / math.sqrt(WIDTH)
    score_scale = 1.0 / math.sqrt(WIDTH)
    tops[...] = jnp.full(tops.shape, MASKED, jnp.float32)
    totals[...] = jnp.zeros(totals.shape, jnp.float32)
    weighted[...] = jnp.zeros(weighted.shape, jnp.float32)

    def head(ref, h):
        return ref[:, h * WIDTH : (h + 1) * WIDTH]

    def scores(k):
        block = keys[k]
        for h in range(HEADS):
            raw = lax.dot_general(
                block, head(q_ref, h), (((1,), (1,)), ((), ())), preferred_element_type=jnp.float32
            )
            raw = raw * to_log2 + bias[k]
            top = jnp.max(raw, axis=0, keepdims=True)
            grown = jnp.exp2(raw - top)
            tops[k, h : h + 1, :] = top
            totals[k, h : h + 1, :] = jnp.sum(grown, axis=0, keepdims=True)
            weights[k, h] = grown
        keys_turned[k] = block.T

    def grad_dots(k):
        block = values[k]
        for h in range(HEADS):
            dot = lax.dot_general(
                block, head(o_ref, h), (((1,), (1,)), ((), ())), preferred_element_type=jnp.float32
            )
            dots[k, h] = dot
            weighted[k, h : h + 1, :] = jnp.sum(weights[k, h] * dot, axis=0, keepdims=True)

    def when_reached(k, *steps):
        @pl.when(depth >= k)
        def _():
            for step in steps:
                step()

    def arrive(k, c):
        def step():
            if k == REACH:
                from_relay(c).wait_recv()
            else:
                forward(k - 1, c).wait_recv()
                if k < REACH - 1:
                    send_forward(k, c)

        return step

    loads[1].wait()
    loads[3].wait()
    scores(0)
    loads[2].wait()
    loads[4].wait()
    grad_dots(0)

    when_reached(1, arrive(1, 0), arrive(1, 1))
    relay(0)
    when_reached(1, arrive(1, 2), arrive(1, 3))
    relay(1)
    when_reached(1, lambda: scores(1))
    when_reached(2, arrive(2, 0), arrive(2, 1))
    relay(2)
    when_reached(1, lambda: grad_dots(1))
    when_reached(2, arrive(2, 2), arrive(2, 3))
    relay(3)
    when_reached(2, lambda: scores(2))
    when_reached(3, arrive(3, 0), arrive(3, 1), lambda: grad_dots(2), lambda: scores(3))

    @pl.when(depth == 2)
    def _():
        grad_dots(2)

    when_reached(3, arrive(3, 2), arrive(3, 3), lambda: grad_dots(3))
    when_reached(4, arrive(4, 0), arrive(4, 1), lambda: scores(4), arrive(4, 2), arrive(4, 3), lambda: grad_dots(4))

    top = tops[0]
    for k in range(1, REACH + 1):
        top = jnp.maximum(top, tops[k])
    total = jnp.zeros_like(top)
    weight = jnp.zeros_like(top)
    for k in range(REACH + 1):
        factor = jnp.exp2(tops[k] - top)
        factors[k] = factor
        total = total + factor * totals[k]
        weight = weight + factor * weighted[k]
    inverse = 1.0 / total
    deltas[...] = weight * inverse
    for k in range(REACH + 1):
        factors[k] = factors[k] * inverse
    dq_acc[...] = jnp.zeros(dq_acc.shape, jnp.float32)

    def gradients(k):
        key_sum = jnp.zeros((ROWS, WIDTH), jnp.float32)
        value_sum = jnp.zeros((ROWS, WIDTH), jnp.float32)
        for h in range(HEADS):
            soft = weights[k, h] * factors[k, h : h + 1, :]
            score_grad = soft * (dots[k, h] - deltas[h : h + 1, :])
            soft_low = soft.astype(jnp.bfloat16)
            grad_low = score_grad.astype(jnp.bfloat16)
            value_sum = value_sum + jnp.dot(soft_low, head(o_ref, h), preferred_element_type=jnp.float32)
            key_sum = key_sum + jnp.dot(grad_low, head(q_ref, h), preferred_element_type=jnp.float32)
            dq_acc[h] += jnp.dot(keys_turned[k], grad_low, preferred_element_type=jnp.float32)
        value_part[...] = value_sum
        key_part[...] = key_sum

    own_parts = (value_part, key_part)

    def send_back(k, c):
        part, rows = piece(c)
        return remote(
            send_box.at[k, part, rows], recv_box.at[k - 1, part, rows], grad_send_sem.at[k, c], grad_recv_sem.at[k - 1, c], left
        )

    def back_to_relay(c):
        part, rows = piece(c)
        return remote(
            send_box.at[REACH, part, rows], passing_back.at[part, rows], far_send_sem.at[2, c], far_recv_sem.at[2, c], back_relay
        )

    def back_from_relay(c):
        part, rows = piece(c)
        return remote(
            passing_back.at[part, rows], far_box.at[part, rows], far_send_sem.at[3, c], far_recv_sem.at[3, c], back_relay_to
        )

    def relay_back(condition, chunks):
        @pl.when(condition)
        def _():
            for c in chunks:
                back_to_relay(c).wait_recv()
                back_from_relay(c).start()

    def pass_back(k):
        for c in range(CHUNKS):
            part, rows = piece(c)
            own = own_parts[part]
            if k < REACH - 1:

                @pl.when(has_right)
                def _(c=c, part=part, rows=rows, own=own):
                    send_back(k + 1, c).wait_recv()
                    own[rows] += recv_box[k, part, rows].astype(jnp.float32)

            send_box[k, part, rows] = own[rows].astype(jnp.bfloat16)
            (back_to_relay(c) if k == REACH else send_back(k, c)).start()

    for k in (3, 4, 2):
        when_reached(k, lambda k=k: gradients(k), lambda k=k: pass_back(k))
    relay_back((me >= 4) & (me < 8), (0, 1))
    when_reached(1, lambda: gradients(1), lambda: pass_back(1))
    relay_back((me >= 4) & (me < 8), (2, 3))
    gradients(0)
    for h in range(HEADS):
        dq_out[:, h * WIDTH : (h + 1) * WIDTH] = (dq_acc[h] * score_scale).T.astype(jnp.bfloat16)

    @pl.when(has_right)
    def _():
        for c in range(CHUNKS):
            part, rows = piece(c)
            send_back(1, c).wait_recv()
            own_parts[part][rows] += recv_box[0, part, rows].astype(jnp.float32)

    relay_back(me < 4, range(CHUNKS))

    @pl.when(in_back)
    def _():
        for c in range(CHUNKS):
            part, rows = piece(c)
            back_from_relay(c).wait_recv()
            own_parts[part][rows] += far_box[part, rows].astype(jnp.float32)

    dv_out[...] = value_part[...].astype(jnp.bfloat16)
    dk_out[...] = (key_part[...] * score_scale).astype(jnp.bfloat16)

    def sent(condition, copy):
        @pl.when(condition)
        def _():
            for c in range(CHUNKS):
                copy(c).wait_send()

    for k in range(REACH - 1):
        sent(has_right & (depth >= k), functools.partial(forward, k))
        sent(depth >= k + 1, functools.partial(send_back, k + 1))
    sent(out_far, to_relay)
    sent(is_relay, from_relay)
    sent(back_far, back_to_relay)
    sent(is_back_relay, back_from_relay)


def store_kernel(dq, dk, dv, dq_out, dk_out, dv_out, sem):
    copies = [
        pltpu.make_async_copy(dq, dq_out, sem.at[0]),
        pltpu.make_async_copy(dk, dk_out, sem.at[1]),
        pltpu.make_async_copy(dv, dv_out, sem.at[2]),
    ]
    for copy in copies:
        copy.start()
    for copy in copies:
        copy.wait()


def shards(query_rows, key_rows, value_rows, out_grad, doc_lengths):
    bf16, f32 = jnp.bfloat16, jnp.float32
    blocks = REACH + 1
    in_hbm = pl.BlockSpec(memory_space=pltpu.HBM)
    in_vmem = pl.BlockSpec(memory_space=pltpu.VMEM)
    operands = [
        pltpu.with_memory_space_constraint(array, pltpu.HBM)
        for array in (doc_lengths, query_rows, key_rows, value_rows, out_grad)
    ]
    results = tuple(jax.ShapeDtypeStruct(array.shape, bf16) for array in (query_rows, key_rows, value_rows))
    gradients = pl.pallas_call(
        attention_kernel,
        out_shape=results,
        in_specs=[in_hbm] * 5,
        out_specs=(in_vmem, in_vmem, in_vmem),
        scratch_shapes=[
            pltpu.SMEM((DOCS,), jnp.int32),
            pltpu.VMEM((ROWS, HEADS * WIDTH), bf16),
            pltpu.VMEM((ROWS, HEADS * WIDTH), bf16),
            pltpu.VMEM((blocks, ROWS, WIDTH), bf16),
            pltpu.VMEM((blocks, ROWS, WIDTH), bf16),
            pltpu.VMEM((2, ROWS, WIDTH), bf16),
            pltpu.VMEM((blocks, WIDTH, ROWS), bf16),
            pltpu.VMEM((blocks, ROWS, ROWS), f32),
            pltpu.VMEM((blocks, HEADS, ROWS, ROWS), f32),
            pltpu.VMEM((blocks, HEADS, ROWS, ROWS), f32),
            pltpu.VMEM((blocks, HEADS, ROWS), f32),
            pltpu.VMEM((blocks, HEADS, ROWS), f32),
            pltpu.VMEM((blocks, HEADS, ROWS), f32),
            pltpu.VMEM((blocks, HEADS, ROWS), f32),
            pltpu.VMEM((HEADS, ROWS), f32),
            pltpu.VMEM((HEADS, WIDTH, ROWS), f32),
            pltpu.VMEM((ROWS, WIDTH), f32),
            pltpu.VMEM((ROWS, WIDTH), f32),
            pltpu.VMEM((blocks, 2, ROWS, WIDTH), bf16),
            pltpu.VMEM((blocks, 2, ROWS, WIDTH), bf16),
            pltpu.VMEM((2, ROWS, WIDTH), bf16),
            pltpu.VMEM((2, ROWS, WIDTH), bf16),
            pltpu.SemaphoreType.DMA((5,)),
            pltpu.SemaphoreType.DMA((REACH, CHUNKS)),
            pltpu.SemaphoreType.DMA((REACH, CHUNKS)),
            pltpu.SemaphoreType.DMA((REACH, CHUNKS)),
            pltpu.SemaphoreType.DMA((REACH, CHUNKS)),
            pltpu.SemaphoreType.DMA((4, CHUNKS)),
            pltpu.SemaphoreType.DMA((4, CHUNKS)),
        ],
        compiler_params=pltpu.CompilerParams(
            collective_id=0, has_side_effects=True, vmem_limit_bytes=48 * 1024 * 1024
        ),
    )(*operands)
    return pl.pallas_call(
        store_kernel,
        out_shape=results,
        in_specs=[in_vmem] * 3,
        out_specs=[in_hbm] * 3,
        scratch_shapes=[pltpu.SemaphoreType.DMA((3,))],
    )(*gradients)


def solution(mesh):
    rows = P(("dp", "ctx"), None)
    return jax.shard_map(
        shards,
        mesh=mesh,
        in_specs=(rows, rows, rows, rows, P("dp")),
        out_specs=(rows, rows, rows),
        check_vma=False,
    )
```

```python
import functools
import math

import jax
import jax.numpy as jnp
from jax import lax
from jax.experimental import pallas as pl
from jax.experimental.pallas import tpu as pltpu
from jax.sharding import PartitionSpec as P

MESH = pl.DeviceIdType.MESH
MASKED = -1e30
HEADS = 8
WIDTH = 128
ROWS = 256
HALF = ROWS // 2
REACH = 4
FIRST = 4
DOCS = 16
CHUNKS = 4
FAR = ()


def attention_kernel(
    lengths_hbm,
    q_hbm,
    k_hbm,
    v_hbm,
    o_hbm,
    dq_out,
    dk_out,
    dv_out,
    lengths,
    q_ref,
    o_ref,
    keys,
    values,
    passing,
    keys_turned,
    bias,
    weights,
    dots,
    tops,
    totals,
    weighted,
    factors,
    deltas,
    dq_acc,
    key_part,
    value_part,
    send_box,
    recv_box,
    far_box,
    passing_back,
    load_sem,
    kv_send_sem,
    kv_recv_sem,
    grad_send_sem,
    grad_recv_sem,
    far_send_sem,
    far_recv_sem,
):
    me = lax.axis_index("ctx")
    size = 16
    depth = jnp.where(me < FIRST, me, me - FIRST)
    has_left = depth > 0
    has_right = (me != FIRST - 1) & (me != size - 1)
    left = jnp.maximum(me - 1, 0)
    right = jnp.minimum(me + 1, size - 1)

    out_far = ((me >= 4) & (me < 12)) & bool(FAR)
    out_relay = jnp.where(me < 6, me - 2, jnp.where(me < 10, me + 6, me - 10))
    is_relay = ((me < 4) | (me >= 12)) & bool(FAR)
    relay_from = jnp.where(me < 2, me + 10, jnp.where(me < 4, me + 2, me - 6))
    relay_to = jnp.where(me < 2, me + 14, jnp.where(me < 4, me + 6, me - 2))
    in_far = (me >= 8) & bool(FAR)
    in_relay = jnp.where(me < 10, me - 6, jnp.where(me < 14, me + 2, me - 14))
    back_far = (me >= 8) & bool(FAR)
    back_relay = jnp.where(me < 14, me - 6, me - 14)
    is_back_relay = (me < 8) & bool(FAR)
    back_relay_from = jnp.where(me < 2, me + 14, me + 6)
    back_relay_to = jnp.where(me < 2, me + 10, me + 2)
    in_back = ((me >= 4) & (me < 12)) & bool(FAR)
    in_back_relay = jnp.where(me < 10, me - 2, me - 10)

    loads = [
        pltpu.make_async_copy(lengths_hbm, lengths, load_sem.at[4]),
        pltpu.make_async_copy(k_hbm, keys.at[0], load_sem.at[0]),
        pltpu.make_async_copy(v_hbm, values.at[0], load_sem.at[1]),
        pltpu.make_async_copy(q_hbm, q_ref, load_sem.at[2]),
        pltpu.make_async_copy(o_hbm, o_ref, load_sem.at[3]),
    ]
    for load in loads:
        load.start()

    barrier = pltpu.get_barrier_semaphore()

    def greet(condition, device):
        @pl.when(condition)
        def _():
            pl.semaphore_signal(barrier, inc=1, device_id={"ctx": device}, device_id_type=MESH)

    greet(has_left, left)
    greet(has_right, right)
    greet(is_relay, relay_from)
    greet(in_far, in_relay)
    greet(is_back_relay, back_relay_from)
    greet(in_back, in_back_relay)
    targets = (has_left, has_right, out_far, is_relay, back_far, is_back_relay)
    pl.semaphore_wait(barrier, sum(target.astype(jnp.int32) for target in targets))

    def remote(source, target, send, recv, device):
        return pltpu.make_async_remote_copy(
            src_ref=source, dst_ref=target, send_sem=send, recv_sem=recv, device_id={"ctx": device}, device_id_type=MESH
        )

    def piece(c):
        return c // 2, pl.ds((c % 2) * HALF, HALF)

    def own_piece(c):
        part, rows = piece(c)
        return (k_hbm, v_hbm)[part].at[rows]

    def forward(k, c):
        part, rows = piece(c)
        place = (keys, values)[part]
        source = own_piece(c) if k == 0 else place.at[k, rows]
        return remote(source, place.at[k + 1, rows], kv_send_sem.at[k, c], kv_recv_sem.at[k + 1, c], right)

    def to_relay(c):
        part, rows = piece(c)
        return remote(own_piece(c), passing.at[part, rows], far_send_sem.at[0, c], far_recv_sem.at[0, c], out_relay)

    def from_relay(c):
        part, rows = piece(c)
        target = (keys, values)[part].at[REACH, rows]
        return remote(passing.at[part, rows], target, far_send_sem.at[1, c], far_recv_sem.at[1, c], relay_to)

    def send_forward(k, c):
        @pl.when(has_right & (depth >= k))
        def _():
            forward(k, c).start()

    def relay(c):
        if c in FAR:

            @pl.when(is_relay)
            def _():
                to_relay(c).wait_recv()
                from_relay(c).start()

    for c in range(CHUNKS):
        send_forward(0, c)
        if c in FAR:

            @pl.when(out_far)
            def _(c=c):
                to_relay(c).start()

    loads[0].wait()
    places = me * ROWS + lax.broadcasted_iota(jnp.int32, (8, ROWS), 1)
    starts = jnp.zeros((8, ROWS), jnp.int32)
    end = jnp.int32(0)
    for d in range(DOCS):
        end = end + lengths[d]
        starts = jnp.where(places >= end, end, starts)
    places, starts = places[:1], starts[:1]
    for k in range(REACH + 1):
        key_places = (me - k) * ROWS + lax.broadcasted_iota(jnp.int32, (ROWS, ROWS), 0)
        allowed = (key_places >= starts) & (key_places <= places)
        bias[k] = jnp.where(allowed, 0.0, MASKED)

    to_log2 = math.log2(math.e) / math.sqrt(WIDTH)
    score_scale = 1.0 / math.sqrt(WIDTH)
    tops[...] = jnp.full(tops.shape, MASKED, jnp.float32)
    totals[...] = jnp.zeros(totals.shape, jnp.float32)
    weighted[...] = jnp.zeros(weighted.shape, jnp.float32)

    def head(ref, h):
        return ref[:, h * WIDTH : (h + 1) * WIDTH]

    def scores(k):
        block = keys[k]
        for h in range(HEADS):
            raw = lax.dot_general(
                block, head(q_ref, h), (((1,), (1,)), ((), ())), preferred_element_type=jnp.float32
            )
            raw = raw * to_log2 + bias[k]
            top = jnp.max(raw, axis=0, keepdims=True)
            grown = jnp.exp2(raw - top)
            tops[k, h : h + 1, :] = top
            totals[k, h : h + 1, :] = jnp.sum(grown, axis=0, keepdims=True)
            weights[k, h] = grown
        keys_turned[k] = block.T

    def grad_dots(k):
        block = values[k]
        for h in range(HEADS):
            dot = lax.dot_general(
                block, head(o_ref, h), (((1,), (1,)), ((), ())), preferred_element_type=jnp.float32
            )
            dots[k, h] = dot
            weighted[k, h : h + 1, :] = jnp.sum(weights[k, h] * dot, axis=0, keepdims=True)

    def when_reached(k, *steps):
        @pl.when(depth >= k)
        def _():
            for step in steps:
                step()

    def arrive(k, c):
        def step():
            if k == REACH and c in FAR:
                from_relay(c).wait_recv()
            else:
                forward(k - 1, c).wait_recv()
                if k < REACH - 1 or (k == REACH - 1 and c not in FAR):
                    send_forward(k, c)

        return step

    loads[1].wait()
    loads[3].wait()
    scores(0)
    loads[2].wait()
    loads[4].wait()
    grad_dots(0)

    when_reached(1, arrive(1, 0), arrive(1, 1))
    relay(0)
    when_reached(1, arrive(1, 2), arrive(1, 3))
    relay(1)
    when_reached(1, lambda: scores(1))
    when_reached(2, arrive(2, 0), arrive(2, 1))
    relay(2)
    when_reached(1, lambda: grad_dots(1))
    when_reached(2, arrive(2, 2), arrive(2, 3))
    relay(3)
    when_reached(2, lambda: scores(2))
    when_reached(3, arrive(3, 0), arrive(3, 1), lambda: grad_dots(2), lambda: scores(3))

    @pl.when(depth == 2)
    def _():
        grad_dots(2)

    when_reached(3, arrive(3, 2), arrive(3, 3), lambda: grad_dots(3))
    when_reached(4, arrive(4, 0), arrive(4, 1), lambda: scores(4), arrive(4, 2), arrive(4, 3), lambda: grad_dots(4))

    top = tops[0]
    for k in range(1, REACH + 1):
        top = jnp.maximum(top, tops[k])
    total = jnp.zeros_like(top)
    weight = jnp.zeros_like(top)
    for k in range(REACH + 1):
        factor = jnp.exp2(tops[k] - top)
        factors[k] = factor
        total = total + factor * totals[k]
        weight = weight + factor * weighted[k]
    inverse = 1.0 / total
    deltas[...] = weight * inverse
    for k in range(REACH + 1):
        factors[k] = factors[k] * inverse
    dq_acc[...] = jnp.zeros(dq_acc.shape, jnp.float32)

    def gradients(k):
        key_sum = jnp.zeros((ROWS, WIDTH), jnp.float32)
        value_sum = jnp.zeros((ROWS, WIDTH), jnp.float32)
        for h in range(HEADS):
            soft = weights[k, h] * factors[k, h : h + 1, :]
            score_grad = soft * (dots[k, h] - deltas[h : h + 1, :])
            soft_low = soft.astype(jnp.bfloat16)
            grad_low = score_grad.astype(jnp.bfloat16)
            value_sum = value_sum + jnp.dot(soft_low, head(o_ref, h), preferred_element_type=jnp.float32)
            key_sum = key_sum + jnp.dot(grad_low, head(q_ref, h), preferred_element_type=jnp.float32)
            dq_acc[h] += jnp.dot(keys_turned[k], grad_low, preferred_element_type=jnp.float32)
        value_part[...] = value_sum
        key_part[...] = key_sum

    own_parts = (value_part, key_part)

    def send_back(k, c):
        part, rows = piece(c)
        return remote(
            send_box.at[k, part, rows], recv_box.at[k - 1, part, rows], grad_send_sem.at[k, c], grad_recv_sem.at[k - 1, c], left
        )

    def back_to_relay(c):
        part, rows = piece(c)
        return remote(
            send_box.at[REACH, part, rows], passing_back.at[part, rows], far_send_sem.at[2, c], far_recv_sem.at[2, c], back_relay
        )

    def back_from_relay(c):
        part, rows = piece(c)
        return remote(
            passing_back.at[part, rows], far_box.at[part, rows], far_send_sem.at[3, c], far_recv_sem.at[3, c], back_relay_to
        )

    def relay_back(condition, chunks):
        @pl.when(condition)
        def _():
            for c in chunks:
                if c in FAR:
                    back_to_relay(c).wait_recv()
                    back_from_relay(c).start()

    def pass_back(k):
        for c in range(CHUNKS):
            part, rows = piece(c)
            own = own_parts[part]
            if k < REACH - 1 or (k == REACH - 1 and c not in FAR):

                @pl.when(has_right & (depth + 1 > k))
                def _(c=c, part=part, rows=rows, own=own):
                    send_back(k + 1, c).wait_recv()
                    own[rows] += recv_box[k, part, rows].astype(jnp.float32)

            send_box[k, part, rows] = own[rows].astype(jnp.bfloat16)
            (back_to_relay(c) if k == REACH and c in FAR else send_back(k, c)).start()

    for k in (4, 3, 2):
        when_reached(k, lambda k=k: gradients(k), lambda k=k: pass_back(k))
    relay_back((me >= 4) & (me < 8), (0, 1))
    when_reached(1, lambda: gradients(1), lambda: pass_back(1))
    relay_back((me >= 4) & (me < 8), (2, 3))
    gradients(0)
    for h in range(HEADS):
        dq_out[:, h * WIDTH : (h + 1) * WIDTH] = (dq_acc[h] * score_scale).T.astype(jnp.bfloat16)

    @pl.when(has_right)
    def _():
        for c in range(CHUNKS):
            part, rows = piece(c)
            send_back(1, c).wait_recv()
            own_parts[part][rows] += recv_box[0, part, rows].astype(jnp.float32)

    relay_back(me < 4, range(CHUNKS))

    @pl.when(in_back)
    def _():
        for c in FAR:
            part, rows = piece(c)
            back_from_relay(c).wait_recv()
            own_parts[part][rows] += far_box[part, rows].astype(jnp.float32)

    dv_out[...] = value_part[...].astype(jnp.bfloat16)
    dk_out[...] = (key_part[...] * score_scale).astype(jnp.bfloat16)

    def sent(condition, copy, chunks):
        @pl.when(condition)
        def _():
            for c in chunks:
                copy(c).wait_send()

    for k in range(REACH):
        chunks = [c for c in range(CHUNKS) if k < REACH - 1 or c not in FAR]
        sent(has_right & (depth >= k), functools.partial(forward, k), chunks)
        sent(depth >= k + 1, functools.partial(send_back, k + 1), chunks)
    sent(out_far, to_relay, FAR)
    sent(is_relay, from_relay, FAR)
    sent(back_far, back_to_relay, FAR)
    sent(is_back_relay, back_from_relay, FAR)


def store_kernel(dq, dk, dv, dq_out, dk_out, dv_out, sem):
    copies = [
        pltpu.make_async_copy(dq, dq_out, sem.at[0]),
        pltpu.make_async_copy(dk, dk_out, sem.at[1]),
        pltpu.make_async_copy(dv, dv_out, sem.at[2]),
    ]
    for copy in copies:
        copy.start()
    for copy in copies:
        copy.wait()


def shards(query_rows, key_rows, value_rows, out_grad, doc_lengths):
    bf16, f32 = jnp.bfloat16, jnp.float32
    blocks = REACH + 1
    in_hbm = pl.BlockSpec(memory_space=pltpu.HBM)
    in_vmem = pl.BlockSpec(memory_space=pltpu.VMEM)
    operands = [
        pltpu.with_memory_space_constraint(array, pltpu.HBM)
        for array in (doc_lengths, query_rows, key_rows, value_rows, out_grad)
    ]
    results = tuple(jax.ShapeDtypeStruct(array.shape, bf16) for array in (query_rows, key_rows, value_rows))
    gradients = pl.pallas_call(
        attention_kernel,
        out_shape=results,
        in_specs=[in_hbm] * 5,
        out_specs=(in_vmem, in_vmem, in_vmem),
        scratch_shapes=[
            pltpu.SMEM((DOCS,), jnp.int32),
            pltpu.VMEM((ROWS, HEADS * WIDTH), bf16),
            pltpu.VMEM((ROWS, HEADS * WIDTH), bf16),
            pltpu.VMEM((blocks, ROWS, WIDTH), bf16),
            pltpu.VMEM((blocks, ROWS, WIDTH), bf16),
            pltpu.VMEM((2, ROWS, WIDTH), bf16),
            pltpu.VMEM((blocks, WIDTH, ROWS), bf16),
            pltpu.VMEM((blocks, ROWS, ROWS), f32),
            pltpu.VMEM((blocks, HEADS, ROWS, ROWS), f32),
            pltpu.VMEM((blocks, HEADS, ROWS, ROWS), f32),
            pltpu.VMEM((blocks, HEADS, ROWS), f32),
            pltpu.VMEM((blocks, HEADS, ROWS), f32),
            pltpu.VMEM((blocks, HEADS, ROWS), f32),
            pltpu.VMEM((blocks, HEADS, ROWS), f32),
            pltpu.VMEM((HEADS, ROWS), f32),
            pltpu.VMEM((HEADS, WIDTH, ROWS), f32),
            pltpu.VMEM((ROWS, WIDTH), f32),
            pltpu.VMEM((ROWS, WIDTH), f32),
            pltpu.VMEM((blocks, 2, ROWS, WIDTH), bf16),
            pltpu.VMEM((blocks, 2, ROWS, WIDTH), bf16),
            pltpu.VMEM((2, ROWS, WIDTH), bf16),
            pltpu.VMEM((2, ROWS, WIDTH), bf16),
            pltpu.SemaphoreType.DMA((5,)),
            pltpu.SemaphoreType.DMA((blocks, CHUNKS)),
            pltpu.SemaphoreType.DMA((blocks, CHUNKS)),
            pltpu.SemaphoreType.DMA((blocks, CHUNKS)),
            pltpu.SemaphoreType.DMA((blocks, CHUNKS)),
            pltpu.SemaphoreType.DMA((4, CHUNKS)),
            pltpu.SemaphoreType.DMA((4, CHUNKS)),
        ],
        compiler_params=pltpu.CompilerParams(
            collective_id=0, has_side_effects=True, vmem_limit_bytes=48 * 1024 * 1024
        ),
    )(*operands)
    gradients = [pltpu.with_memory_space_constraint(g, pltpu.VMEM) for g in gradients]
    return pl.pallas_call(
        store_kernel,
        out_shape=results,
        in_specs=[in_vmem] * 3,
        out_specs=[in_hbm] * 3,
        scratch_shapes=[pltpu.SemaphoreType.DMA((3,))],
    )(*gradients)


def solution(mesh):
    rows = P(("dp", "ctx"), None)
    return jax.shard_map(
        shards,
        mesh=mesh,
        in_specs=(rows, rows, rows, rows, P("dp")),
        out_specs=(rows, rows, rows),
        check_vma=False,
    )
```

```python
import functools
import math

import jax
import jax.numpy as jnp
from jax import lax
from jax.experimental import pallas as pl
from jax.experimental.pallas import tpu as pltpu
from jax.sharding import PartitionSpec as P

MESH = pl.DeviceIdType.MESH
MASKED = -1e30
HEADS = 8
WIDTH = 128
ROWS = 256
HALF = ROWS // 2
REACH = 4
FIRST = 4
DOCS = 16
CHUNKS = 4


def attention_kernel(
    lengths_hbm,
    q_hbm,
    k_hbm,
    v_hbm,
    o_hbm,
    dq_out,
    dk_out,
    dv_out,
    lengths,
    q_ref,
    o_ref,
    keys,
    values,
    picked,
    passing,
    keys_turned,
    bias,
    weights,
    dots,
    tops,
    totals,
    weighted,
    factors,
    deltas,
    dq_acc,
    key_part,
    value_part,
    send_box,
    recv_box,
    far_box,
    pair_box,
    load_sem,
    kv_send_sem,
    kv_recv_sem,
    grad_send_sem,
    grad_recv_sem,
    far_send_sem,
    far_recv_sem,
):
    me = lax.axis_index("ctx")
    size = 16
    depth = jnp.where(me < FIRST, me, me - FIRST)
    has_left = depth > 0
    has_right = (me != FIRST - 1) & (me != size - 1)
    left = jnp.maximum(me - 1, 0)
    right = jnp.minimum(me + 1, size - 1)

    odd = me % 2 == 1
    picks = odd & (me >= 5) & (me <= 11)
    pick_relay = jnp.where(me == 5, 10, jnp.where(me == 7, 5, jnp.where(me == 9, 14, 0)))
    is_relay = (me == 10) | (me == 5) | (me == 14) | (me == 0)
    picked_on = jnp.where(me == 10, 5, jnp.where(me == 5, 7, jnp.where(me == 14, 9, 11)))
    relay_to = jnp.where(me == 0, 15, jnp.where(me == 5, 11, me - 1))
    in_relay = jnp.where(me < 10, 10, jnp.where(me < 12, 5, jnp.where(me < 14, 14, 0)))
    is_far = me >= 8
    owns_far = (me >= 4) & (me < 12)

    loads = [
        pltpu.make_async_copy(lengths_hbm, lengths, load_sem.at[4]),
        pltpu.make_async_copy(k_hbm, keys.at[0], load_sem.at[0]),
        pltpu.make_async_copy(v_hbm, values.at[0], load_sem.at[1]),
        pltpu.make_async_copy(q_hbm, q_ref, load_sem.at[2]),
        pltpu.make_async_copy(o_hbm, o_ref, load_sem.at[3]),
    ]
    for load in loads:
        load.start()

    barrier = pltpu.get_barrier_semaphore()

    def greet(condition, device):
        @pl.when(condition)
        def _():
            pl.semaphore_signal(barrier, inc=1, device_id={"ctx": device}, device_id_type=MESH)

    greet(has_left, left)
    greet(has_right, right)
    greet(is_relay, picked_on)
    greet(is_far & (me != 9) & (me != 13), in_relay)
    targets = (has_left, has_right, picks, is_relay, (me == 0) | (me == 5))
    pl.semaphore_wait(barrier, sum(target.astype(jnp.int32) for target in targets))

    def remote(source, target, send, recv, device):
        return pltpu.make_async_remote_copy(
            src_ref=source, dst_ref=target, send_sem=send, recv_sem=recv, device_id={"ctx": device}, device_id_type=MESH
        )

    def piece(c):
        return c // 2, pl.ds((c % 2) * HALF, HALF)

    def own_piece(c):
        part, rows = piece(c)
        return (k_hbm, v_hbm)[part].at[rows]

    def forward(k, c):
        part, rows = piece(c)
        place = (keys, values)[part]
        source = own_piece(c) if k == 0 else place.at[k, rows]
        return remote(source, place.at[k + 1, rows], kv_send_sem.at[k, c], kv_recv_sem.at[k + 1, c], right)

    def to_relay(c):
        part, rows = piece(c)
        return remote(
            picked.at[part, rows], passing.at[part, rows], far_send_sem.at[0, c], far_recv_sem.at[0, c], pick_relay
        )

    def from_relay(c, which):
        part, rows = piece(c)
        return remote(
            passing.at[part, rows],
            (keys, values)[part].at[REACH, rows],
            far_send_sem.at[1 + which, c],
            far_recv_sem.at[1, c],
            relay_to - which,
        )

    def send_forward(k, c):
        @pl.when(has_right & (depth >= k))
        def _():
            forward(k, c).start()

    def relay(c):
        @pl.when(is_relay)
        def _():
            to_relay(c).wait_recv()
            for which in (1, 0):
                from_relay(c, which).start()

    for c in range(CHUNKS):
        send_forward(0, c)

    loads[0].wait()
    places = me * ROWS + lax.broadcasted_iota(jnp.int32, (8, ROWS), 1)
    starts = jnp.zeros((8, ROWS), jnp.int32)
    end = jnp.int32(0)
    for d in range(DOCS):
        end = end + lengths[d]
        starts = jnp.where(places >= end, end, starts)
    places, starts = places[:1], starts[:1]
    for k in range(REACH + 1):
        key_places = (me - k) * ROWS + lax.broadcasted_iota(jnp.int32, (ROWS, ROWS), 0)
        allowed = (key_places >= starts) & (key_places <= places)
        bias[k] = jnp.where(allowed, 0.0, MASKED)

    def far_in_use(block):
        start, end = jnp.int32(0), jnp.int32(0)
        for d in range(DOCS):
            end = end + lengths[d]
            start = jnp.where(end <= (block + REACH) * ROWS, end, start)
        return jnp.full((HALF, WIDTH), start, jnp.int32) < (block + 1) * ROWS

    to_log2 = math.log2(math.e) / math.sqrt(WIDTH)
    score_scale = 1.0 / math.sqrt(WIDTH)
    tops[...] = jnp.full(tops.shape, MASKED, jnp.float32)
    totals[...] = jnp.zeros(totals.shape, jnp.float32)
    weighted[...] = jnp.zeros(weighted.shape, jnp.float32)

    def head(ref, h):
        return ref[:, h * WIDTH : (h + 1) * WIDTH]

    def scores(k):
        block = keys[k]
        for h in range(HEADS):
            raw = lax.dot_general(
                block, head(q_ref, h), (((1,), (1,)), ((), ())), preferred_element_type=jnp.float32
            )
            raw = raw * to_log2 + bias[k]
            top = jnp.max(raw, axis=0, keepdims=True)
            grown = jnp.exp2(raw - top)
            tops[k, h : h + 1, :] = top
            totals[k, h : h + 1, :] = jnp.sum(grown, axis=0, keepdims=True)
            weights[k, h] = grown
        keys_turned[k] = block.T

    def grad_dots(k):
        block = values[k]
        for h in range(HEADS):
            dot = lax.dot_general(
                block, head(o_ref, h), (((1,), (1,)), ((), ())), preferred_element_type=jnp.float32
            )
            dots[k, h] = dot
            weighted[k, h : h + 1, :] = jnp.sum(weights[k, h] * dot, axis=0, keepdims=True)

    def when_reached(k, *steps):
        @pl.when(depth >= k)
        def _():
            for step in steps:
                step()

    def arrive(k, c):
        def step():
            if k == REACH:
                from_relay(c, 0).wait_recv()
            else:
                forward(k - 1, c).wait_recv()
                if k < REACH - 1:
                    send_forward(k, c)

        return step

    def pick(c):
        part, rows = piece(c)
        place = (keys, values)[part]
        before, own = (place[k, rows].astype(jnp.float32) for k in (1, 0))
        picked[part, rows] = jnp.where(far_in_use(me - 1), before, own).astype(jnp.bfloat16)
        to_relay(c).start()

    loads[1].wait()
    loads[3].wait()
    scores(0)
    loads[2].wait()
    loads[4].wait()
    grad_dots(0)

    for c in range(CHUNKS):
        when_reached(1, arrive(1, c))

        @pl.when(picks)
        def _(c=c):
            pick(c)

    when_reached(1, lambda: scores(1))
    relay(0)
    when_reached(2, arrive(2, 0), arrive(2, 1))
    relay(1)
    when_reached(2, arrive(2, 2))
    relay(2)
    when_reached(2, arrive(2, 3))
    relay(3)
    when_reached(1, lambda: grad_dots(1))
    when_reached(2, lambda: scores(2))
    when_reached(3, arrive(3, 0), arrive(3, 1), lambda: scores(3))
    when_reached(2, lambda: grad_dots(2))
    when_reached(4, arrive(4, 0), arrive(4, 1), lambda: scores(4))
    when_reached(3, arrive(3, 2), arrive(3, 3), lambda: grad_dots(3))
    when_reached(4, arrive(4, 2), arrive(4, 3), lambda: grad_dots(4))

    top = tops[0]
    for k in range(1, REACH + 1):
        top = jnp.maximum(top, tops[k])
    total = jnp.zeros_like(top)
    weight = jnp.zeros_like(top)
    for k in range(REACH + 1):
        factor = jnp.exp2(tops[k] - top)
        factors[k] = factor
        total = total + factor * totals[k]
        weight = weight + factor * weighted[k]
    inverse = 1.0 / total
    deltas[...] = weight * inverse
    for k in range(REACH + 1):
        factors[k] = factors[k] * inverse
    dq_acc[...] = jnp.zeros(dq_acc.shape, jnp.float32)

    def gradients(k):
        key_sum = jnp.zeros((ROWS, WIDTH), jnp.float32)
        value_sum = jnp.zeros((ROWS, WIDTH), jnp.float32)
        for h in range(HEADS):
            soft = weights[k, h] * factors[k, h : h + 1, :]
            score_grad = soft * (dots[k, h] - deltas[h : h + 1, :])
            soft_low = soft.astype(jnp.bfloat16)
            grad_low = score_grad.astype(jnp.bfloat16)
            value_sum = value_sum + jnp.dot(soft_low, head(o_ref, h), preferred_element_type=jnp.float32)
            key_sum = key_sum + jnp.dot(grad_low, head(q_ref, h), preferred_element_type=jnp.float32)
            dq_acc[h] += jnp.dot(keys_turned[k], grad_low, preferred_element_type=jnp.float32)
        value_part[...] = value_sum
        key_part[...] = key_sum

    own_parts = (value_part, key_part)

    def send_back(k, c):
        part, rows = piece(c)
        return remote(
            send_box.at[k, part, rows], recv_box.at[k - 1, part, rows], grad_send_sem.at[k, c], grad_recv_sem.at[k - 1, c], left
        )

    def far_pair(c):
        part, rows = piece(c)
        return remote(
            send_box.at[REACH, part, rows], pair_box.at[part, rows], far_send_sem.at[3, c], far_recv_sem.at[2, c], right
        )

    def far_back(c):
        part, rows = piece(c)
        return remote(
            send_box.at[REACH, part, rows], far_box.at[part, rows], far_send_sem.at[3, c], far_recv_sem.at[3, c], me - 5
        )

    def far_on(c):
        part, rows = piece(c)
        return remote(far_box.at[part, rows], far_box.at[part, rows], far_send_sem.at[4, c], far_recv_sem.at[4, c], right)

    def send_far():
        for c in range(CHUNKS):
            part, rows = piece(c)
            send_box[REACH, part, rows] = own_parts[part][rows].astype(jnp.bfloat16)

            @pl.when(jnp.logical_not(odd))
            def _(c=c):
                far_pair(c).start()

    def add_pair(c):
        @pl.when(is_far & odd)
        def _():
            part, rows = piece(c)
            far_pair(c).wait_recv()
            pair = send_box[REACH, part, rows].astype(jnp.float32) + pair_box[part, rows].astype(jnp.float32)
            send_box[REACH, part, rows] = pair.astype(jnp.bfloat16)
            far_back(c).start()

    def pass_far(c):
        @pl.when(owns_far & jnp.logical_not(odd))
        def _():
            far_back(c).wait_recv()
            far_on(c).start()

    def pass_back(k, c):
        part, rows = piece(c)
        own = own_parts[part]
        if k < REACH - 1:

            @pl.when(has_right)
            def _():
                send_back(k + 1, c).wait_recv()
                own[rows] += recv_box[k, part, rows].astype(jnp.float32)

        send_box[k, part, rows] = own[rows].astype(jnp.bfloat16)
        send_back(k, c).start()

    when_reached(4, lambda: gradients(4), send_far)
    when_reached(3, lambda: gradients(3), *[functools.partial(pass_back, 3, c) for c in range(CHUNKS)])
    when_reached(2, lambda: gradients(2))
    for c in range(CHUNKS):
        add_pair(c)
        when_reached(2, functools.partial(pass_back, 2, c))
    when_reached(1, lambda: gradients(1))
    for c in range(CHUNKS):
        when_reached(1, functools.partial(pass_back, 1, c))
        pass_far(c)
    gradients(0)
    for h in range(HEADS):
        dq_out[:, h * WIDTH : (h + 1) * WIDTH] = (dq_acc[h] * score_scale).T.astype(jnp.bfloat16)

    @pl.when(has_right)
    def _():
        for c in range(CHUNKS):
            part, rows = piece(c)
            send_back(1, c).wait_recv()
            own_parts[part][rows] += recv_box[0, part, rows].astype(jnp.float32)

    @pl.when(owns_far)
    def _():
        in_use = far_in_use(me)
        for c in range(CHUNKS):
            part, rows = piece(c)

            @pl.when(odd)
            def _(c=c):
                far_on(c).wait_recv()

            own_parts[part][rows] += jnp.where(in_use, far_box[part, rows].astype(jnp.float32), 0.0)

    dv_out[...] = value_part[...].astype(jnp.bfloat16)
    dk_out[...] = (key_part[...] * score_scale).astype(jnp.bfloat16)

    def sent(condition, copy):
        @pl.when(condition)
        def _():
            for c in range(CHUNKS):
                copy(c).wait_send()

    for k in range(REACH - 1):
        sent(has_right & (depth >= k), functools.partial(forward, k))
        sent(depth >= k + 1, functools.partial(send_back, k + 1))
    sent(picks, to_relay)
    sent(is_relay, functools.partial(from_relay, which=0))
    sent(is_relay, functools.partial(from_relay, which=1))
    sent(is_far & jnp.logical_not(odd), far_pair)
    sent(is_far & odd, far_back)
    sent(owns_far & jnp.logical_not(odd), far_on)


def store_kernel(dq, dk, dv, dq_out, dk_out, dv_out, sem):
    copies = [
        pltpu.make_async_copy(dq, dq_out, sem.at[0]),
        pltpu.make_async_copy(dk, dk_out, sem.at[1]),
        pltpu.make_async_copy(dv, dv_out, sem.at[2]),
    ]
    for copy in copies:
        copy.start()
    for copy in copies:
        copy.wait()


def shards(query_rows, key_rows, value_rows, out_grad, doc_lengths):
    bf16, f32 = jnp.bfloat16, jnp.float32
    blocks = REACH + 1
    in_hbm = pl.BlockSpec(memory_space=pltpu.HBM)
    in_vmem = pl.BlockSpec(memory_space=pltpu.VMEM)
    operands = [
        pltpu.with_memory_space_constraint(array, pltpu.HBM)
        for array in (doc_lengths, query_rows, key_rows, value_rows, out_grad)
    ]
    results = tuple(jax.ShapeDtypeStruct(array.shape, bf16) for array in (query_rows, key_rows, value_rows))
    gradients = pl.pallas_call(
        attention_kernel,
        out_shape=results,
        in_specs=[in_hbm] * 5,
        out_specs=(in_vmem, in_vmem, in_vmem),
        scratch_shapes=[
            pltpu.SMEM((DOCS,), jnp.int32),
            pltpu.VMEM((ROWS, HEADS * WIDTH), bf16),
            pltpu.VMEM((ROWS, HEADS * WIDTH), bf16),
            pltpu.VMEM((blocks, ROWS, WIDTH), bf16),
            pltpu.VMEM((blocks, ROWS, WIDTH), bf16),
            pltpu.VMEM((2, ROWS, WIDTH), bf16),
            pltpu.VMEM((2, ROWS, WIDTH), bf16),
            pltpu.VMEM((blocks, WIDTH, ROWS), bf16),
            pltpu.VMEM((blocks, ROWS, ROWS), f32),
            pltpu.VMEM((blocks, HEADS, ROWS, ROWS), f32),
            pltpu.VMEM((blocks, HEADS, ROWS, ROWS), f32),
            pltpu.VMEM((blocks, HEADS, ROWS), f32),
            pltpu.VMEM((blocks, HEADS, ROWS), f32),
            pltpu.VMEM((blocks, HEADS, ROWS), f32),
            pltpu.VMEM((blocks, HEADS, ROWS), f32),
            pltpu.VMEM((HEADS, ROWS), f32),
            pltpu.VMEM((HEADS, WIDTH, ROWS), f32),
            pltpu.VMEM((ROWS, WIDTH), f32),
            pltpu.VMEM((ROWS, WIDTH), f32),
            pltpu.VMEM((blocks, 2, ROWS, WIDTH), bf16),
            pltpu.VMEM((blocks, 2, ROWS, WIDTH), bf16),
            pltpu.VMEM((2, ROWS, WIDTH), bf16),
            pltpu.VMEM((2, ROWS, WIDTH), bf16),
            pltpu.SemaphoreType.DMA((5,)),
            pltpu.SemaphoreType.DMA((blocks, CHUNKS)),
            pltpu.SemaphoreType.DMA((blocks, CHUNKS)),
            pltpu.SemaphoreType.DMA((blocks, CHUNKS)),
            pltpu.SemaphoreType.DMA((blocks, CHUNKS)),
            pltpu.SemaphoreType.DMA((5, CHUNKS)),
            pltpu.SemaphoreType.DMA((5, CHUNKS)),
        ],
        compiler_params=pltpu.CompilerParams(
            collective_id=0, has_side_effects=True, vmem_limit_bytes=48 * 1024 * 1024
        ),
    )(*operands)
    gradients = [pltpu.with_memory_space_constraint(g, pltpu.VMEM) for g in gradients]
    return pl.pallas_call(
        store_kernel,
        out_shape=results,
        in_specs=[in_vmem] * 3,
        out_specs=[in_hbm] * 3,
        scratch_shapes=[pltpu.SemaphoreType.DMA((3,))],
    )(*gradients)


def solution(mesh):
    rows = P(("dp", "ctx"), None)
    return jax.shard_map(
        shards,
        mesh=mesh,
        in_specs=(rows, rows, rows, rows, P("dp")),
        out_specs=(rows, rows, rows),
        check_vma=False,
    )
```

```python
import functools
import math

import jax
import jax.numpy as jnp
from jax import lax
from jax.experimental import pallas as pl
from jax.experimental.pallas import tpu as pltpu
from jax.sharding import PartitionSpec as P

MESH = pl.DeviceIdType.MESH
MASKED = -1e30
HEADS = 8
WIDTH = 128
ROWS = 256
REACH = 4
FIRST = 4
DOCS = 16
PIECES = 2
CHUNKS = 2 * PIECES
SLICE = ROWS // PIECES


def attention_kernel(
    lengths_hbm,
    q_hbm,
    k_hbm,
    v_hbm,
    o_hbm,
    dq_out,
    dk_out,
    dv_out,
    lengths,
    q_ref,
    o_ref,
    keys,
    values,
    picked,
    passing,
    keys_turned,
    bias,
    weights,
    dots,
    tops,
    totals,
    weighted,
    factors,
    deltas,
    dq_acc,
    key_part,
    value_part,
    send_box,
    recv_box,
    far_box,
    pair_box,
    load_sem,
    kv_send_sem,
    kv_recv_sem,
    grad_send_sem,
    grad_recv_sem,
    far_send_sem,
    far_recv_sem,
    far_ready,
):
    me = lax.axis_index("ctx")
    size = 16
    depth = jnp.where(me < FIRST, me, me - FIRST)
    has_left = depth > 0
    has_right = (me != FIRST - 1) & (me != size - 1)
    left = jnp.maximum(me - 1, 0)
    right = jnp.minimum(me + 1, size - 1)

    odd = me % 2 == 1
    picks = odd & (me >= 5) & (me <= 11)
    pick_relay = jnp.where(me == 5, 10, jnp.where(me == 7, 5, jnp.where(me == 9, 14, 0)))
    is_relay = (me == 10) | (me == 5) | (me == 14) | (me == 0)
    relay_to = jnp.where(me == 0, 15, jnp.where(me == 5, 11, me - 1))
    is_far = me >= 8
    owns_far = (me >= 4) & (me < 12)

    barrier = pltpu.get_barrier_semaphore()

    def greet(condition, device):
        @pl.when(condition)
        def _():
            pl.semaphore_signal(barrier, inc=1, device_id={"ctx": device}, device_id_type=MESH)

    greet(has_left, left)
    greet((me == 10) | (me == 11), 5)
    greet(me == 5, 6)
    greet(me == 8, 10)
    greet(me == 9, 14)
    greet(me == 0, 11)
    greet((me == 14) | (me == 15), 0)

    loads = [
        pltpu.make_async_copy(lengths_hbm, lengths, load_sem.at[4]),
        pltpu.make_async_copy(k_hbm, keys.at[0], load_sem.at[0]),
        pltpu.make_async_copy(v_hbm, values.at[0], load_sem.at[1]),
        pltpu.make_async_copy(q_hbm, q_ref, load_sem.at[2]),
        pltpu.make_async_copy(o_hbm, o_ref, load_sem.at[3]),
    ]
    for load in loads:
        load.start()

    expected = has_right.astype(jnp.int32)
    for device, more in ((0, 2), (5, 2), (6, 1), (10, 1), (11, 1), (14, 1)):
        expected += jnp.where(me == device, more, 0)

    @pl.when(has_right)
    def _():
        pl.semaphore_wait(barrier, expected)

    @pl.when(me == 14)
    def _():
        pl.semaphore_signal(far_ready, inc=1, device_id={"ctx": 9}, device_id_type=MESH)

    def remote(source, target, send, recv, device):
        return pltpu.make_async_remote_copy(
            src_ref=source, dst_ref=target, send_sem=send, recv_sem=recv, device_id={"ctx": device}, device_id_type=MESH
        )

    def piece(c):
        return c // PIECES, pl.ds((c % PIECES) * SLICE, SLICE)

    def own_piece(c):
        part, rows = piece(c)
        return (k_hbm, v_hbm)[part].at[rows]

    def forward(k, c):
        part, rows = piece(c)
        place = (keys, values)[part]
        source = own_piece(c) if k == 0 else place.at[k, rows]
        return remote(source, place.at[k + 1, rows], kv_send_sem.at[k, c], kv_recv_sem.at[k + 1, c], right)

    def to_relay(c):
        part, rows = piece(c)
        return remote(
            picked.at[part, rows], passing.at[part, rows], far_send_sem.at[0, c], far_recv_sem.at[0, c], pick_relay
        )

    def from_relay(c, which):
        part, rows = piece(c)
        return remote(
            passing.at[part, rows],
            (keys, values)[part].at[REACH, rows],
            far_send_sem.at[1 + which, c],
            far_recv_sem.at[1, c],
            relay_to - which,
        )

    def send_forward(k, c):
        @pl.when(has_right & (depth >= k))
        def _():
            forward(k, c).start()

    def relay(c):
        @pl.when(is_relay)
        def _():
            to_relay(c).wait_recv()
            for which in (1, 0):
                from_relay(c, which).start()

    for c in range(CHUNKS):
        send_forward(0, c)

    loads[0].wait()
    places = me * ROWS + lax.broadcasted_iota(jnp.int32, (8, ROWS), 1)
    starts = jnp.zeros((8, ROWS), jnp.int32)
    end = jnp.int32(0)
    for d in range(DOCS):
        end = end + lengths[d]
        starts = jnp.where(places >= end, end, starts)
    places, starts = places[:1], starts[:1]
    for k in range(REACH + 1):
        key_places = (me - k) * ROWS + lax.broadcasted_iota(jnp.int32, (ROWS, ROWS), 0)
        allowed = (key_places >= starts) & (key_places <= places)
        bias[k] = jnp.where(allowed, 0.0, MASKED)

    def far_in_use(block):
        start, end = jnp.int32(0), jnp.int32(0)
        for d in range(DOCS):
            end = end + lengths[d]
            start = jnp.where(end <= (block + REACH) * ROWS, end, start)
        return jnp.full((SLICE, WIDTH), start, jnp.int32) < (block + 1) * ROWS

    to_log2 = math.log2(math.e) / math.sqrt(WIDTH)
    score_scale = 1.0 / math.sqrt(WIDTH)
    tops[...] = jnp.full(tops.shape, MASKED, jnp.float32)
    totals[...] = jnp.zeros(totals.shape, jnp.float32)
    weighted[...] = jnp.zeros(weighted.shape, jnp.float32)

    def head(ref, h):
        return ref[:, h * WIDTH : (h + 1) * WIDTH]

    def scores(k):
        block = keys[k]
        for h in range(HEADS):
            raw = lax.dot_general(
                block, head(q_ref, h), (((1,), (1,)), ((), ())), preferred_element_type=jnp.float32
            )
            raw = raw * to_log2 + bias[k]
            top = jnp.max(raw, axis=0, keepdims=True)
            grown = jnp.exp2(raw - top)
            tops[k, h : h + 1, :] = top
            totals[k, h : h + 1, :] = jnp.sum(grown, axis=0, keepdims=True)
            weights[k, h] = grown
        keys_turned[k] = block.T

    def grad_dots(k):
        block = values[k]
        for h in range(HEADS):
            dot = lax.dot_general(
                block, head(o_ref, h), (((1,), (1,)), ((), ())), preferred_element_type=jnp.float32
            )
            dots[k, h] = dot
            weighted[k, h : h + 1, :] = jnp.sum(weights[k, h] * dot, axis=0, keepdims=True)

    def when_reached(k, *steps):
        @pl.when(depth >= k)
        def _():
            for step in steps:
                step()

    def arrive(k, c):
        def step():
            if k == REACH:
                from_relay(c, 0).wait_recv()
            else:
                forward(k - 1, c).wait_recv()
                if k < REACH - 1:
                    send_forward(k, c)

        return step

    def pick(c):
        part, rows = piece(c)
        place = (keys, values)[part]
        before, own = (place[k, rows].astype(jnp.float32) for k in (1, 0))
        picked[part, rows] = jnp.where(far_in_use(me - 1), before, own).astype(jnp.bfloat16)
        if c == 0:

            @pl.when(me == 9)
            def _():
                pl.semaphore_wait(far_ready, 1)

        to_relay(c).start()

    loads[1].wait()
    loads[3].wait()
    scores(0)
    loads[2].wait()
    loads[4].wait()
    grad_dots(0)

    for c in range(CHUNKS):
        when_reached(1, arrive(1, c))

        @pl.when(picks)
        def _(c=c):
            pick(c)

    first, second = range(PIECES), range(PIECES, CHUNKS)
    when_reached(1, lambda: scores(1))
    for c in range(CHUNKS):
        when_reached(2, arrive(2, c))
        relay(c)
    when_reached(1, lambda: grad_dots(1))
    when_reached(2, lambda: scores(2))
    when_reached(3, *[arrive(3, c) for c in first], lambda: scores(3))
    when_reached(2, lambda: grad_dots(2))
    when_reached(4, *[arrive(4, c) for c in first], lambda: scores(4))
    when_reached(3, *[arrive(3, c) for c in second], lambda: grad_dots(3))
    when_reached(4, *[arrive(4, c) for c in second], lambda: grad_dots(4))

    top = tops[0]
    for k in range(1, REACH + 1):
        top = jnp.maximum(top, tops[k])
    total = jnp.zeros_like(top)
    weight = jnp.zeros_like(top)
    for k in range(REACH + 1):
        factor = jnp.exp2(tops[k] - top)
        factors[k] = factor
        total = total + factor * totals[k]
        weight = weight + factor * weighted[k]
    inverse = 1.0 / total
    deltas[...] = weight * inverse
    for k in range(REACH + 1):
        factors[k] = factors[k] * inverse
    dq_acc[...] = jnp.zeros(dq_acc.shape, jnp.float32)

    def value_gradients(k):
        value_sum = jnp.zeros((ROWS, WIDTH), jnp.float32)
        for h in range(HEADS):
            soft_low = (weights[k, h] * factors[k, h : h + 1, :]).astype(jnp.bfloat16)
            value_sum = value_sum + jnp.dot(soft_low, head(o_ref, h), preferred_element_type=jnp.float32)
        value_part[...] = value_sum

    def key_gradients(k):
        key_sum = jnp.zeros((ROWS, WIDTH), jnp.float32)
        for h in range(HEADS):
            soft = weights[k, h] * factors[k, h : h + 1, :]
            grad_low = (soft * (dots[k, h] - deltas[h : h + 1, :])).astype(jnp.bfloat16)
            key_sum = key_sum + jnp.dot(grad_low, head(q_ref, h), preferred_element_type=jnp.float32)
            dq_acc[h] += jnp.dot(keys_turned[k], grad_low, preferred_element_type=jnp.float32)
        key_part[...] = key_sum

    def gradients(k):
        value_gradients(k)
        key_gradients(k)

    own_parts = (value_part, key_part)

    def send_back(k, c):
        part, rows = piece(c)
        return remote(
            send_box.at[k, part, rows], recv_box.at[k - 1, part, rows], grad_send_sem.at[k, c], grad_recv_sem.at[k - 1, c], left
        )

    def far_pair(c):
        part, rows = piece(c)
        return remote(
            send_box.at[REACH, part, rows], pair_box.at[part, rows], far_send_sem.at[3, c], far_recv_sem.at[2, c], right
        )

    def far_back(c):
        part, rows = piece(c)
        return remote(
            send_box.at[REACH, part, rows], far_box.at[part, rows], far_send_sem.at[3, c], far_recv_sem.at[3, c], me - 5
        )

    def far_on(c):
        part, rows = piece(c)
        return remote(far_box.at[part, rows], far_box.at[part, rows], far_send_sem.at[4, c], far_recv_sem.at[4, c], right)

    def add_pair(c):
        @pl.when(is_far & odd)
        def _():
            part, rows = piece(c)
            far_pair(c).wait_recv()
            pair = send_box[REACH, part, rows].astype(jnp.float32) + pair_box[part, rows].astype(jnp.float32)
            send_box[REACH, part, rows] = pair.astype(jnp.bfloat16)
            far_back(c).start()

    def pass_far(c):
        @pl.when(owns_far & jnp.logical_not(odd))
        def _():
            far_back(c).wait_recv()
            far_on(c).start()

    def pass_back(k, c):
        part, rows = piece(c)
        own = own_parts[part]
        if k < REACH - 1:

            @pl.when(has_right)
            def _():
                send_back(k + 1, c).wait_recv()
                own[rows] += recv_box[k, part, rows].astype(jnp.float32)

        send_box[k, part, rows] = own[rows].astype(jnp.bfloat16)
        send_back(k, c).start()

    def passed(k, chunks):
        return [functools.partial(pass_back, k, c) for c in chunks]

    def send_far(chunks):
        for c in chunks:
            part, rows = piece(c)
            send_box[REACH, part, rows] = own_parts[part][rows].astype(jnp.bfloat16)

            @pl.when(jnp.logical_not(odd))
            def _(c=c):
                far_pair(c).start()

    when_reached(3, lambda: value_gradients(3), *passed(3, first))
    when_reached(4, lambda: value_gradients(4), lambda: send_far(first))
    when_reached(3, lambda: key_gradients(3), *passed(3, second))
    when_reached(4, lambda: key_gradients(4), lambda: send_far(second))
    when_reached(2, lambda: gradients(2), *passed(2, first))
    for c in first:
        add_pair(c)
    when_reached(2, *passed(2, second))
    when_reached(1, lambda: gradients(1))
    for c in second:
        add_pair(c)
    when_reached(1, *passed(1, range(CHUNKS)))
    for c in first:
        pass_far(c)
    gradients(0)
    for c in second:
        pass_far(c)
    for h in range(HEADS):
        dq_out[:, h * WIDTH : (h + 1) * WIDTH] = (dq_acc[h] * score_scale).T.astype(jnp.bfloat16)

    @pl.when(has_right)
    def _():
        for c in range(CHUNKS):
            part, rows = piece(c)
            send_back(1, c).wait_recv()
            own_parts[part][rows] += recv_box[0, part, rows].astype(jnp.float32)

    @pl.when(owns_far)
    def _():
        in_use = far_in_use(me)
        for c in range(CHUNKS):
            part, rows = piece(c)

            @pl.when(odd)
            def _(c=c):
                far_on(c).wait_recv()

            own_parts[part][rows] += jnp.where(in_use, far_box[part, rows].astype(jnp.float32), 0.0)

    dv_out[...] = value_part[...].astype(jnp.bfloat16)
    dk_out[...] = (key_part[...] * score_scale).astype(jnp.bfloat16)

    def sent(condition, copy):
        @pl.when(condition)
        def _():
            for c in range(CHUNKS):
                copy(c).wait_send()

    for k in range(REACH - 1):
        sent(has_right & (depth >= k), functools.partial(forward, k))
        sent(depth >= k + 1, functools.partial(send_back, k + 1))
    sent(picks, to_relay)
    sent(is_relay, functools.partial(from_relay, which=0))
    sent(is_relay, functools.partial(from_relay, which=1))
    sent(is_far & jnp.logical_not(odd), far_pair)
    sent(is_far & odd, far_back)
    sent(owns_far & jnp.logical_not(odd), far_on)


def store_kernel(dq, dk, dv, dq_out, dk_out, dv_out, sem):
    copies = [
        pltpu.make_async_copy(dq, dq_out, sem.at[0]),
        pltpu.make_async_copy(dk, dk_out, sem.at[1]),
        pltpu.make_async_copy(dv, dv_out, sem.at[2]),
    ]
    for copy in copies:
        copy.start()
    for copy in copies:
        copy.wait()


def shards(query_rows, key_rows, value_rows, out_grad, doc_lengths):
    bf16, f32 = jnp.bfloat16, jnp.float32
    blocks = REACH + 1
    in_hbm = pl.BlockSpec(memory_space=pltpu.HBM)
    in_vmem = pl.BlockSpec(memory_space=pltpu.VMEM)
    operands = [
        pltpu.with_memory_space_constraint(array, pltpu.HBM)
        for array in (doc_lengths, query_rows, key_rows, value_rows, out_grad)
    ]
    results = tuple(jax.ShapeDtypeStruct(array.shape, bf16) for array in (query_rows, key_rows, value_rows))
    gradients = pl.pallas_call(
        attention_kernel,
        out_shape=results,
        in_specs=[in_hbm] * 5,
        out_specs=(in_vmem, in_vmem, in_vmem),
        scratch_shapes=[
            pltpu.SMEM((DOCS,), jnp.int32),
            pltpu.VMEM((ROWS, HEADS * WIDTH), bf16),
            pltpu.VMEM((ROWS, HEADS * WIDTH), bf16),
            pltpu.VMEM((blocks, ROWS, WIDTH), bf16),
            pltpu.VMEM((blocks, ROWS, WIDTH), bf16),
            pltpu.VMEM((2, ROWS, WIDTH), bf16),
            pltpu.VMEM((2, ROWS, WIDTH), bf16),
            pltpu.VMEM((blocks, WIDTH, ROWS), bf16),
            pltpu.VMEM((blocks, ROWS, ROWS), f32),
            pltpu.VMEM((blocks, HEADS, ROWS, ROWS), f32),
            pltpu.VMEM((blocks, HEADS, ROWS, ROWS), f32),
            pltpu.VMEM((blocks, HEADS, ROWS), f32),
            pltpu.VMEM((blocks, HEADS, ROWS), f32),
            pltpu.VMEM((blocks, HEADS, ROWS), f32),
            pltpu.VMEM((blocks, HEADS, ROWS), f32),
            pltpu.VMEM((HEADS, ROWS), f32),
            pltpu.VMEM((HEADS, WIDTH, ROWS), f32),
            pltpu.VMEM((ROWS, WIDTH), f32),
            pltpu.VMEM((ROWS, WIDTH), f32),
            pltpu.VMEM((blocks, 2, ROWS, WIDTH), bf16),
            pltpu.VMEM((blocks, 2, ROWS, WIDTH), bf16),
            pltpu.VMEM((2, ROWS, WIDTH), bf16),
            pltpu.VMEM((2, ROWS, WIDTH), bf16),
            pltpu.SemaphoreType.DMA((5,)),
            pltpu.SemaphoreType.DMA((blocks, CHUNKS)),
            pltpu.SemaphoreType.DMA((blocks, CHUNKS)),
            pltpu.SemaphoreType.DMA((blocks, CHUNKS)),
            pltpu.SemaphoreType.DMA((blocks, CHUNKS)),
            pltpu.SemaphoreType.DMA((5, CHUNKS)),
            pltpu.SemaphoreType.DMA((5, CHUNKS)),
            pltpu.SemaphoreType.REGULAR,
        ],
        compiler_params=pltpu.CompilerParams(
            collective_id=0, has_side_effects=True, vmem_limit_bytes=48 * 1024 * 1024
        ),
    )(*operands)
    gradients = [pltpu.with_memory_space_constraint(g, pltpu.VMEM) for g in gradients]
    return pl.pallas_call(
        store_kernel,
        out_shape=results,
        in_specs=[in_vmem] * 3,
        out_specs=[in_hbm] * 3,
        scratch_shapes=[pltpu.SemaphoreType.DMA((3,))],
    )(*gradients)


def solution(mesh):
    rows = P(("dp", "ctx"), None)
    return jax.shard_map(
        shards,
        mesh=mesh,
        in_specs=(rows, rows, rows, rows, P("dp")),
        out_specs=(rows, rows, rows),
        check_vma=False,
    )
```

```python
import functools
import math

import jax
import jax.numpy as jnp
from jax import lax
from jax.experimental import pallas as pl
from jax.experimental.pallas import tpu as pltpu
from jax.sharding import PartitionSpec as P

MESH = pl.DeviceIdType.MESH
MASKED = -1e30
HEADS = 8
WIDTH = 128
ROWS = 256
REACH = 4
FIRST = 4
DOCS = 16
PIECES = 2
CHUNKS = 2 * PIECES
SLICE = ROWS // PIECES


def attention_kernel(
    lengths_hbm,
    q_hbm,
    k_hbm,
    v_hbm,
    o_hbm,
    dq_out,
    dk_out,
    dv_out,
    lengths,
    q_ref,
    o_ref,
    keys,
    values,
    picked,
    passing,
    keys_turned,
    bias,
    weights,
    dots,
    tops,
    totals,
    weighted,
    factors,
    deltas,
    dq_acc,
    key_part,
    value_part,
    send_box,
    recv_box,
    far_box,
    pair_box,
    load_sem,
    kv_send_sem,
    kv_recv_sem,
    grad_send_sem,
    grad_recv_sem,
    far_send_sem,
    far_recv_sem,
    far_ready,
):
    me = lax.axis_index("ctx")
    size = 16
    depth = jnp.where(me < FIRST, me, me - FIRST)
    has_left = depth > 0
    has_right = (me != FIRST - 1) & (me != size - 1)
    left = jnp.maximum(me - 1, 0)
    right = jnp.minimum(me + 1, size - 1)

    odd = me % 2 == 1
    picks = odd & (me >= 5) & (me <= 11)
    pick_relay = jnp.where(me == 5, 10, jnp.where(me == 7, 5, jnp.where(me == 9, 14, 0)))
    is_relay = (me == 10) | (me == 5) | (me == 14) | (me == 0)
    relay_to = jnp.where(me == 0, 15, jnp.where(me == 5, 11, me - 1))
    is_far = me >= 8
    owns_far = (me >= 4) & (me < 12)

    barrier = pltpu.get_barrier_semaphore()

    def greet(condition, device):
        @pl.when(condition)
        def _():
            pl.semaphore_signal(barrier, inc=1, device_id={"ctx": device}, device_id_type=MESH)

    greet(has_left, left)
    greet((me == 10) | (me == 11), 5)
    greet(me == 5, 6)
    greet(me == 8, 10)
    greet(me == 9, 14)
    greet(me == 0, 11)
    greet((me == 14) | (me == 15), 0)

    loads = [
        pltpu.make_async_copy(lengths_hbm, lengths, load_sem.at[4]),
        pltpu.make_async_copy(k_hbm, keys.at[0], load_sem.at[0]),
        pltpu.make_async_copy(v_hbm, values.at[0], load_sem.at[1]),
        pltpu.make_async_copy(q_hbm, q_ref, load_sem.at[2]),
        pltpu.make_async_copy(o_hbm, o_ref, load_sem.at[3]),
    ]
    for load in loads:
        load.start()

    expected = has_right.astype(jnp.int32)
    for device, more in ((0, 2), (5, 2), (6, 1), (10, 1), (11, 1), (14, 1)):
        expected += jnp.where(me == device, more, 0)

    @pl.when(has_right)
    def _():
        pl.semaphore_wait(barrier, expected)

    @pl.when(me == 14)
    def _():
        pl.semaphore_signal(far_ready, inc=1, device_id={"ctx": 9}, device_id_type=MESH)

    def remote(source, target, send, recv, device):
        return pltpu.make_async_remote_copy(
            src_ref=source, dst_ref=target, send_sem=send, recv_sem=recv, device_id={"ctx": device}, device_id_type=MESH
        )

    def piece(c):
        return c // PIECES, pl.ds((c % PIECES) * SLICE, SLICE)

    def own_piece(c):
        part, rows = piece(c)
        return (k_hbm, v_hbm)[part].at[rows]

    def forward(k, c):
        part, rows = piece(c)
        place = (keys, values)[part]
        source = own_piece(c) if k == 0 else place.at[k, rows]
        return remote(source, place.at[k + 1, rows], kv_send_sem.at[k, c], kv_recv_sem.at[k + 1, c], right)

    def to_relay(c):
        part, rows = piece(c)
        return remote(
            picked.at[part, rows], passing.at[part, rows], far_send_sem.at[0, c], far_recv_sem.at[0, c], pick_relay
        )

    def from_relay(c, which):
        part, rows = piece(c)
        return remote(
            passing.at[part, rows],
            (keys, values)[part].at[REACH, rows],
            far_send_sem.at[1 + which, c],
            far_recv_sem.at[1, c],
            relay_to - which,
        )

    def send_forward(k, c):
        @pl.when(has_right & (depth >= k))
        def _():
            forward(k, c).start()

    def relay(c):
        @pl.when(is_relay)
        def _():
            to_relay(c).wait_recv()
            for which in (1, 0):
                from_relay(c, which).start()

    for c in range(CHUNKS):
        send_forward(0, c)

    loads[0].wait()
    places = me * ROWS + lax.broadcasted_iota(jnp.int32, (8, ROWS), 1)
    starts = jnp.zeros((8, ROWS), jnp.int32)
    end = jnp.int32(0)
    for d in range(DOCS):
        end = end + lengths[d]
        starts = jnp.where(places >= end, end, starts)
    places, starts = places[:1], starts[:1]
    for k in range(REACH + 1):
        key_places = (me - k) * ROWS + lax.broadcasted_iota(jnp.int32, (ROWS, ROWS), 0)
        allowed = (key_places >= starts) & (key_places <= places)
        bias[k] = jnp.where(allowed, 0.0, MASKED)

    def far_in_use(block):
        start, end = jnp.int32(0), jnp.int32(0)
        for d in range(DOCS):
            end = end + lengths[d]
            start = jnp.where(end <= (block + REACH) * ROWS, end, start)
        return jnp.full((SLICE, WIDTH), start, jnp.int32) < (block + 1) * ROWS

    to_log2 = math.log2(math.e) / math.sqrt(WIDTH)
    score_scale = 1.0 / math.sqrt(WIDTH)
    tops[...] = jnp.full(tops.shape, MASKED, jnp.float32)
    totals[...] = jnp.zeros(totals.shape, jnp.float32)
    weighted[...] = jnp.zeros(weighted.shape, jnp.float32)

    def head(ref, h):
        return ref[:, h * WIDTH : (h + 1) * WIDTH]

    def scores(k):
        block = keys[k]
        for h in range(HEADS):
            raw = lax.dot_general(
                block, head(q_ref, h), (((1,), (1,)), ((), ())), preferred_element_type=jnp.float32
            )
            raw = raw * to_log2 + bias[k]
            top = jnp.max(raw, axis=0, keepdims=True)
            grown = jnp.exp2(raw - top)
            tops[k, h : h + 1, :] = top
            totals[k, h : h + 1, :] = jnp.sum(grown, axis=0, keepdims=True)
            weights[k, h] = grown
        keys_turned[k] = block.T

    def grad_dots(k):
        block = values[k]
        for h in range(HEADS):
            dot = lax.dot_general(
                block, head(o_ref, h), (((1,), (1,)), ((), ())), preferred_element_type=jnp.float32
            )
            dots[k, h] = dot
            weighted[k, h : h + 1, :] = jnp.sum(weights[k, h] * dot, axis=0, keepdims=True)

    def when_reached(k, *steps):
        @pl.when(depth >= k)
        def _():
            for step in steps:
                step()

    def arrive(k, c):
        def step():
            if k == REACH:
                from_relay(c, 0).wait_recv()
            else:
                forward(k - 1, c).wait_recv()
                if k < REACH - 1:
                    send_forward(k, c)

        return step

    def pick(c):
        part, rows = piece(c)
        place = (keys, values)[part]
        before, own = (place[k, rows].astype(jnp.float32) for k in (1, 0))
        picked[part, rows] = jnp.where(far_in_use(me - 1), before, own).astype(jnp.bfloat16)
        if c == 0:

            @pl.when(me == 9)
            def _():
                pl.semaphore_wait(far_ready, 1)

        to_relay(c).start()

    loads[1].wait()
    loads[3].wait()
    scores(0)
    loads[2].wait()
    loads[4].wait()
    grad_dots(0)

    for c in range(CHUNKS):
        when_reached(1, arrive(1, c))

        @pl.when(picks)
        def _(c=c):
            pick(c)

    first, second = range(PIECES), range(PIECES, CHUNKS)
    when_reached(1, lambda: scores(1))
    for c in range(CHUNKS):
        when_reached(2, arrive(2, c))
        relay(c)
    when_reached(1, lambda: grad_dots(1))
    when_reached(2, lambda: scores(2))
    when_reached(3, *[arrive(3, c) for c in first], lambda: scores(3))
    when_reached(2, lambda: grad_dots(2))
    when_reached(4, *[arrive(4, c) for c in first], lambda: scores(4))
    when_reached(3, *[arrive(3, c) for c in second], lambda: grad_dots(3))
    when_reached(4, *[arrive(4, c) for c in second], lambda: grad_dots(4))

    top = tops[0]
    for k in range(1, REACH + 1):
        top = jnp.maximum(top, tops[k])
    total = jnp.zeros_like(top)
    weight = jnp.zeros_like(top)
    for k in range(REACH + 1):
        factor = jnp.exp2(tops[k] - top)
        factors[k] = factor
        total = total + factor * totals[k]
        weight = weight + factor * weighted[k]
    inverse = 1.0 / total
    deltas[...] = weight * inverse
    for k in range(REACH + 1):
        factors[k] = factors[k] * inverse
    dq_acc[...] = jnp.zeros(dq_acc.shape, jnp.float32)

    def value_gradients(k):
        value_sum = jnp.zeros((ROWS, WIDTH), jnp.float32)
        for h in range(HEADS):
            soft_low = (weights[k, h] * factors[k, h : h + 1, :]).astype(jnp.bfloat16)
            value_sum = value_sum + jnp.dot(soft_low, head(o_ref, h), preferred_element_type=jnp.float32)
        value_part[...] = value_sum

    def key_gradients(k):
        key_sum = jnp.zeros((ROWS, WIDTH), jnp.float32)
        for h in range(HEADS):
            soft = weights[k, h] * factors[k, h : h + 1, :]
            grad_low = (soft * (dots[k, h] - deltas[h : h + 1, :])).astype(jnp.bfloat16)
            key_sum = key_sum + jnp.dot(grad_low, head(q_ref, h), preferred_element_type=jnp.float32)
            dq_acc[h] += jnp.dot(keys_turned[k], grad_low, preferred_element_type=jnp.float32)
        key_part[...] = key_sum

    def gradients(k):
        value_gradients(k)
        key_gradients(k)

    own_parts = (value_part, key_part)

    def send_back(k, c):
        part, rows = piece(c)
        return remote(
            send_box.at[k, part, rows], recv_box.at[k - 1, part, rows], grad_send_sem.at[k, c], grad_recv_sem.at[k - 1, c], left
        )

    def far_pair(c):
        part, rows = piece(c)
        return remote(
            send_box.at[REACH, part, rows], pair_box.at[part, rows], far_send_sem.at[3, c], far_recv_sem.at[2, c], right
        )

    def far_back(c):
        part, rows = piece(c)
        return remote(
            send_box.at[REACH, part, rows], far_box.at[part, rows], far_send_sem.at[3, c], far_recv_sem.at[3, c], me - 5
        )

    def far_on(c):
        part, rows = piece(c)
        return remote(far_box.at[part, rows], far_box.at[part, rows], far_send_sem.at[4, c], far_recv_sem.at[4, c], right)

    def add_pair(c):
        @pl.when(is_far & odd)
        def _():
            part, rows = piece(c)
            far_pair(c).wait_recv()
            pair = send_box[REACH, part, rows].astype(jnp.float32) + pair_box[part, rows].astype(jnp.float32)
            send_box[REACH, part, rows] = pair.astype(jnp.bfloat16)
            far_back(c).start()

    def pass_far(c):
        @pl.when(owns_far & jnp.logical_not(odd))
        def _():
            far_back(c).wait_recv()
            far_on(c).start()

    def pass_back(k, c):
        part, rows = piece(c)
        own = own_parts[part]
        if k < REACH - 1:

            @pl.when(has_right)
            def _():
                send_back(k + 1, c).wait_recv()
                own[rows] += recv_box[k, part, rows].astype(jnp.float32)

        send_box[k, part, rows] = own[rows].astype(jnp.bfloat16)
        send_back(k, c).start()

    def passed(k, chunks):
        return [functools.partial(pass_back, k, c) for c in chunks]

    def send_far(chunks):
        for c in chunks:
            part, rows = piece(c)
            send_box[REACH, part, rows] = own_parts[part][rows].astype(jnp.bfloat16)

            @pl.when(jnp.logical_not(odd))
            def _(c=c):
                far_pair(c).start()

    when_reached(4, lambda: value_gradients(4), lambda: send_far(first))
    when_reached(3, lambda: value_gradients(3), *passed(3, first))
    when_reached(4, lambda: key_gradients(4), lambda: send_far(second))
    when_reached(3, lambda: key_gradients(3), *passed(3, second))
    when_reached(2, lambda: gradients(2))
    for chunks in (first, second):
        for c in chunks:
            add_pair(c)
        when_reached(2, *passed(2, chunks))
    when_reached(1, lambda: gradients(1))
    when_reached(1, *passed(1, range(CHUNKS)))
    for c in first:
        pass_far(c)
    gradients(0)
    for c in second:
        pass_far(c)
    for h in range(HEADS):
        dq_out[:, h * WIDTH : (h + 1) * WIDTH] = (dq_acc[h] * score_scale).T.astype(jnp.bfloat16)

    @pl.when(has_right)
    def _():
        for c in range(CHUNKS):
            part, rows = piece(c)
            send_back(1, c).wait_recv()
            own_parts[part][rows] += recv_box[0, part, rows].astype(jnp.float32)

    @pl.when(owns_far)
    def _():
        in_use = far_in_use(me)
        for c in range(CHUNKS):
            part, rows = piece(c)

            @pl.when(odd)
            def _(c=c):
                far_on(c).wait_recv()

            own_parts[part][rows] += jnp.where(in_use, far_box[part, rows].astype(jnp.float32), 0.0)

    dv_out[...] = value_part[...].astype(jnp.bfloat16)
    dk_out[...] = (key_part[...] * score_scale).astype(jnp.bfloat16)

    def sent(condition, copy):
        @pl.when(condition)
        def _():
            for c in range(CHUNKS):
                copy(c).wait_send()

    for k in range(REACH - 1):
        sent(has_right & (depth >= k), functools.partial(forward, k))
        sent(depth >= k + 1, functools.partial(send_back, k + 1))
    sent(picks, to_relay)
    sent(is_relay, functools.partial(from_relay, which=0))
    sent(is_relay, functools.partial(from_relay, which=1))
    sent(is_far & jnp.logical_not(odd), far_pair)
    sent(is_far & odd, far_back)
    sent(owns_far & jnp.logical_not(odd), far_on)


def store_kernel(dq, dk, dv, dq_out, dk_out, dv_out, sem):
    copies = [
        pltpu.make_async_copy(dq, dq_out, sem.at[0]),
        pltpu.make_async_copy(dk, dk_out, sem.at[1]),
        pltpu.make_async_copy(dv, dv_out, sem.at[2]),
    ]
    for copy in copies:
        copy.start()
    for copy in copies:
        copy.wait()


def shards(query_rows, key_rows, value_rows, out_grad, doc_lengths):
    bf16, f32 = jnp.bfloat16, jnp.float32
    blocks = REACH + 1
    in_hbm = pl.BlockSpec(memory_space=pltpu.HBM)
    in_vmem = pl.BlockSpec(memory_space=pltpu.VMEM)
    operands = [
        pltpu.with_memory_space_constraint(array, pltpu.HBM)
        for array in (doc_lengths, query_rows, key_rows, value_rows, out_grad)
    ]
    results = tuple(jax.ShapeDtypeStruct(array.shape, bf16) for array in (query_rows, key_rows, value_rows))
    gradients = pl.pallas_call(
        attention_kernel,
        out_shape=results,
        in_specs=[in_hbm] * 5,
        out_specs=(in_vmem, in_vmem, in_vmem),
        scratch_shapes=[
            pltpu.SMEM((DOCS,), jnp.int32),
            pltpu.VMEM((ROWS, HEADS * WIDTH), bf16),
            pltpu.VMEM((ROWS, HEADS * WIDTH), bf16),
            pltpu.VMEM((blocks, ROWS, WIDTH), bf16),
            pltpu.VMEM((blocks, ROWS, WIDTH), bf16),
            pltpu.VMEM((2, ROWS, WIDTH), bf16),
            pltpu.VMEM((2, ROWS, WIDTH), bf16),
            pltpu.VMEM((blocks, WIDTH, ROWS), bf16),
            pltpu.VMEM((blocks, ROWS, ROWS), f32),
            pltpu.VMEM((blocks, HEADS, ROWS, ROWS), f32),
            pltpu.VMEM((blocks, HEADS, ROWS, ROWS), f32),
            pltpu.VMEM((blocks, HEADS, ROWS), f32),
            pltpu.VMEM((blocks, HEADS, ROWS), f32),
            pltpu.VMEM((blocks, HEADS, ROWS), f32),
            pltpu.VMEM((blocks, HEADS, ROWS), f32),
            pltpu.VMEM((HEADS, ROWS), f32),
            pltpu.VMEM((HEADS, WIDTH, ROWS), f32),
            pltpu.VMEM((ROWS, WIDTH), f32),
            pltpu.VMEM((ROWS, WIDTH), f32),
            pltpu.VMEM((blocks, 2, ROWS, WIDTH), bf16),
            pltpu.VMEM((blocks, 2, ROWS, WIDTH), bf16),
            pltpu.VMEM((2, ROWS, WIDTH), bf16),
            pltpu.VMEM((2, ROWS, WIDTH), bf16),
            pltpu.SemaphoreType.DMA((5,)),
            pltpu.SemaphoreType.DMA((blocks, CHUNKS)),
            pltpu.SemaphoreType.DMA((blocks, CHUNKS)),
            pltpu.SemaphoreType.DMA((blocks, CHUNKS)),
            pltpu.SemaphoreType.DMA((blocks, CHUNKS)),
            pltpu.SemaphoreType.DMA((5, CHUNKS)),
            pltpu.SemaphoreType.DMA((5, CHUNKS)),
            pltpu.SemaphoreType.REGULAR,
        ],
        compiler_params=pltpu.CompilerParams(
            collective_id=0, has_side_effects=True, vmem_limit_bytes=48 * 1024 * 1024
        ),
    )(*operands)
    gradients = [pltpu.with_memory_space_constraint(g, pltpu.VMEM) for g in gradients]
    return pl.pallas_call(
        store_kernel,
        out_shape=results,
        in_specs=[in_vmem] * 3,
        out_specs=[in_hbm] * 3,
        scratch_shapes=[pltpu.SemaphoreType.DMA((3,))],
    )(*gradients)


def solution(mesh):
    rows = P(("dp", "ctx"), None)
    return jax.shard_map(
        shards,
        mesh=mesh,
        in_specs=(rows, rows, rows, rows, P("dp")),
        out_specs=(rows, rows, rows),
        check_vma=False,
    )
```

```python
import functools
import math

import jax
import jax.numpy as jnp
from jax import lax
from jax.experimental import pallas as pl
from jax.experimental.pallas import tpu as pltpu
from jax.sharding import PartitionSpec as P

MESH = pl.DeviceIdType.MESH
MASKED = -1e30
HEADS = 8
WIDTH = 128
ROWS = 256
REACH = 4
FIRST = 4
DOCS = 16
PIECES = 2
CHUNKS = 2 * PIECES
SLICE = ROWS // PIECES


def attention_kernel(
    lengths_hbm,
    q_hbm,
    k_hbm,
    v_hbm,
    o_hbm,
    dq_out,
    dk_out,
    dv_out,
    lengths,
    q_ref,
    o_ref,
    keys,
    values,
    picked,
    passing,
    keys_turned,
    bias,
    weights,
    dots,
    tops,
    totals,
    weighted,
    factors,
    deltas,
    dq_acc,
    key_part,
    value_part,
    send_box,
    recv_box,
    far_box,
    pair_box,
    load_sem,
    kv_send_sem,
    kv_recv_sem,
    grad_send_sem,
    grad_recv_sem,
    far_send_sem,
    far_recv_sem,
    far_ready,
):
    me = lax.axis_index("ctx")
    size = 16
    depth = jnp.where(me < FIRST, me, me - FIRST)
    has_left = depth > 0
    has_right = (me != FIRST - 1) & (me != size - 1)
    left = jnp.maximum(me - 1, 0)
    right = jnp.minimum(me + 1, size - 1)

    odd = me % 2 == 1
    picks = odd & (me >= 5) & (me <= 11)
    pick_relay = jnp.where(me == 5, 10, jnp.where(me == 7, 5, jnp.where(me == 9, 15, 0)))
    is_relay = (me == 10) | (me == 5) | (me == 15) | (me == 0)
    relay_to = jnp.where(me == 0, 15, jnp.where(me == 5, 11, jnp.where(me == 10, 9, 13)))
    is_far = me >= 8
    owns_far = (me >= 4) & (me < 12)

    barrier = pltpu.get_barrier_semaphore()

    def greet(condition, device):
        @pl.when(condition)
        def _():
            pl.semaphore_signal(barrier, inc=1, device_id={"ctx": device}, device_id_type=MESH)

    greet(has_left, left)
    greet((me == 10) | (me == 11), 5)
    greet(me == 5, 6)
    greet(me == 8, 10)
    greet(me == 9, 15)
    greet((me == 12) | (me == 13), 14)
    greet(me == 0, 11)
    greet((me == 14) | (me == 15), 0)

    loads = [
        pltpu.make_async_copy(lengths_hbm, lengths, load_sem.at[4]),
        pltpu.make_async_copy(k_hbm, keys.at[0], load_sem.at[0]),
        pltpu.make_async_copy(v_hbm, values.at[0], load_sem.at[1]),
        pltpu.make_async_copy(q_hbm, q_ref, load_sem.at[2]),
        pltpu.make_async_copy(o_hbm, o_ref, load_sem.at[3]),
    ]
    for load in loads:
        load.start()

    expected = has_right.astype(jnp.int32)
    for device, more in ((0, 2), (5, 2), (6, 1), (10, 1), (11, 1), (14, 2), (15, 1)):
        expected += jnp.where(me == device, more, 0)

    @pl.when(me != FIRST - 1)
    def _():
        pl.semaphore_wait(barrier, expected)

    @pl.when(me == 15)
    def _():
        pl.semaphore_signal(far_ready, inc=1, device_id={"ctx": 9}, device_id_type=MESH)

    def remote(source, target, send, recv, device):
        return pltpu.make_async_remote_copy(
            src_ref=source, dst_ref=target, send_sem=send, recv_sem=recv, device_id={"ctx": device}, device_id_type=MESH
        )

    def piece(c):
        return c // PIECES, pl.ds((c % PIECES) * SLICE, SLICE)

    def own_piece(c):
        part, rows = piece(c)
        return (k_hbm, v_hbm)[part].at[rows]

    def forward(k, c):
        part, rows = piece(c)
        place = (keys, values)[part]
        source = own_piece(c) if k == 0 else place.at[k, rows]
        return remote(source, place.at[k + 1, rows], kv_send_sem.at[k, c], kv_recv_sem.at[k + 1, c], right)

    def to_relay(c):
        part, rows = piece(c)
        return remote(
            picked.at[part, rows], passing.at[part, rows], far_send_sem.at[0, c], far_recv_sem.at[0, c], pick_relay
        )

    def from_relay(c, which):
        part, rows = piece(c)
        return remote(
            passing.at[part, rows],
            (keys, values)[part].at[REACH, rows],
            far_send_sem.at[1 + which, c],
            far_recv_sem.at[1, c],
            relay_to - which,
        )

    def send_forward(k, c):
        @pl.when(has_right & (depth >= k))
        def _():
            forward(k, c).start()

    def relay(c, condition):
        @pl.when(is_relay & condition)
        def _():
            to_relay(c).wait_recv()
            for which in (1, 0):
                from_relay(c, which).start()

    for c in range(CHUNKS):
        send_forward(0, c)

    loads[0].wait()
    places = me * ROWS + lax.broadcasted_iota(jnp.int32, (8, ROWS), 1)
    starts = jnp.zeros((8, ROWS), jnp.int32)
    end = jnp.int32(0)
    for d in range(DOCS):
        end = end + lengths[d]
        starts = jnp.where(places >= end, end, starts)
    places, starts = places[:1], starts[:1]
    for k in range(REACH + 1):
        key_places = (me - k) * ROWS + lax.broadcasted_iota(jnp.int32, (ROWS, ROWS), 0)
        allowed = (key_places >= starts) & (key_places <= places)
        bias[k] = jnp.where(allowed, 0.0, MASKED)

    def far_in_use(block):
        start, end = jnp.int32(0), jnp.int32(0)
        for d in range(DOCS):
            end = end + lengths[d]
            start = jnp.where(end <= (block + REACH) * ROWS, end, start)
        return jnp.full((SLICE, WIDTH), start, jnp.int32) < (block + 1) * ROWS

    to_log2 = math.log2(math.e) / math.sqrt(WIDTH)
    score_scale = 1.0 / math.sqrt(WIDTH)
    tops[...] = jnp.full(tops.shape, MASKED, jnp.float32)
    totals[...] = jnp.zeros(totals.shape, jnp.float32)
    weighted[...] = jnp.zeros(weighted.shape, jnp.float32)

    def head(ref, h):
        return ref[:, h * WIDTH : (h + 1) * WIDTH]

    def scores(k):
        block = keys[k]
        for h in range(HEADS):
            raw = lax.dot_general(
                block, head(q_ref, h), (((1,), (1,)), ((), ())), preferred_element_type=jnp.float32
            )
            raw = raw * to_log2 + bias[k]
            top = jnp.max(raw, axis=0, keepdims=True)
            grown = jnp.exp2(raw - top)
            tops[k, h : h + 1, :] = top
            totals[k, h : h + 1, :] = jnp.sum(grown, axis=0, keepdims=True)
            weights[k, h] = grown
        keys_turned[k] = block.T

    def grad_dots(k):
        block = values[k]
        for h in range(HEADS):
            dot = lax.dot_general(
                block, head(o_ref, h), (((1,), (1,)), ((), ())), preferred_element_type=jnp.float32
            )
            dots[k, h] = dot
            weighted[k, h : h + 1, :] = jnp.sum(weights[k, h] * dot, axis=0, keepdims=True)

    def when_reached(k, *steps):
        @pl.when(depth >= k)
        def _():
            for step in steps:
                step()

    def arrive(k, c):
        def step():
            if k == REACH:
                from_relay(c, 0).wait_recv()
            else:
                forward(k - 1, c).wait_recv()
                if k < REACH - 1:
                    send_forward(k, c)

        return step

    def pick(c):
        part, rows = piece(c)
        place = (keys, values)[part]
        before, own = (place[k, rows].astype(jnp.float32) for k in (1, 0))
        picked[part, rows] = jnp.where(far_in_use(me - 1), before, own).astype(jnp.bfloat16)
        if c == 0:

            @pl.when(me == 9)
            def _():
                pl.semaphore_wait(far_ready, 1)

        to_relay(c).start()

    loads[1].wait()
    loads[3].wait()
    scores(0)
    loads[2].wait()
    loads[4].wait()
    grad_dots(0)

    for c in range(CHUNKS):
        when_reached(1, arrive(1, c))

        @pl.when(picks)
        def _(c=c):
            pick(c)

    first, second = range(PIECES), range(PIECES, CHUNKS)
    when_reached(1, lambda: scores(1))
    for c in range(CHUNKS):
        relay(c, me != 10)
        when_reached(2, arrive(2, c))
        relay(c, me == 10)
    when_reached(1, lambda: grad_dots(1))
    when_reached(2, lambda: scores(2))
    when_reached(3, *[arrive(3, c) for c in first], lambda: scores(3))
    when_reached(2, lambda: grad_dots(2))
    when_reached(4, *[arrive(4, c) for c in first], lambda: scores(4))
    when_reached(3, *[arrive(3, c) for c in second], lambda: grad_dots(3))
    when_reached(4, *[arrive(4, c) for c in second], lambda: grad_dots(4))

    top = tops[0]
    for k in range(1, REACH + 1):
        top = jnp.maximum(top, tops[k])
    total = jnp.zeros_like(top)
    weight = jnp.zeros_like(top)
    for k in range(REACH + 1):
        factor = jnp.exp2(tops[k] - top)
        factors[k] = factor
        total = total + factor * totals[k]
        weight = weight + factor * weighted[k]
    inverse = 1.0 / total
    deltas[...] = weight * inverse
    for k in range(REACH + 1):
        factors[k] = factors[k] * inverse
    dq_acc[...] = jnp.zeros(dq_acc.shape, jnp.float32)

    def value_gradients(k):
        value_sum = jnp.zeros((ROWS, WIDTH), jnp.float32)
        for h in range(HEADS):
            soft_low = (weights[k, h] * factors[k, h : h + 1, :]).astype(jnp.bfloat16)
            value_sum = value_sum + jnp.dot(soft_low, head(o_ref, h), preferred_element_type=jnp.float32)
        value_part[...] = value_sum

    def key_gradients(k):
        key_sum = jnp.zeros((ROWS, WIDTH), jnp.float32)
        for h in range(HEADS):
            soft = weights[k, h] * factors[k, h : h + 1, :]
            grad_low = (soft * (dots[k, h] - deltas[h : h + 1, :])).astype(jnp.bfloat16)
            key_sum = key_sum + jnp.dot(grad_low, head(q_ref, h), preferred_element_type=jnp.float32)
            dq_acc[h] += jnp.dot(keys_turned[k], grad_low, preferred_element_type=jnp.float32)
        key_part[...] = key_sum

    def gradients(k):
        value_gradients(k)
        key_gradients(k)

    own_parts = (value_part, key_part)

    def send_back(k, c):
        part, rows = piece(c)
        return remote(
            send_box.at[k, part, rows], recv_box.at[k - 1, part, rows], grad_send_sem.at[k, c], grad_recv_sem.at[k - 1, c], left
        )

    def far_pair(c):
        part, rows = piece(c)
        return remote(
            send_box.at[REACH, part, rows], pair_box.at[part, rows], far_send_sem.at[3, c], far_recv_sem.at[2, c], right
        )

    def far_back(c):
        part, rows = piece(c)
        return remote(
            send_box.at[REACH, part, rows], far_box.at[part, rows], far_send_sem.at[3, c], far_recv_sem.at[3, c], me - 5
        )

    def far_on(c):
        part, rows = piece(c)
        return remote(far_box.at[part, rows], far_box.at[part, rows], far_send_sem.at[4, c], far_recv_sem.at[4, c], right)

    def add_pair(c):
        @pl.when(is_far & odd)
        def _():
            part, rows = piece(c)
            far_pair(c).wait_recv()
            pair = send_box[REACH, part, rows].astype(jnp.float32) + pair_box[part, rows].astype(jnp.float32)
            send_box[REACH, part, rows] = pair.astype(jnp.bfloat16)
            far_back(c).start()

    def pass_far(c):
        @pl.when(owns_far & jnp.logical_not(odd))
        def _():
            far_back(c).wait_recv()
            far_on(c).start()

    def pass_back(k, c):
        part, rows = piece(c)
        own = own_parts[part]
        if k < REACH - 1:

            @pl.when(has_right)
            def _():
                send_back(k + 1, c).wait_recv()
                own[rows] += recv_box[k, part, rows].astype(jnp.float32)

        send_box[k, part, rows] = own[rows].astype(jnp.bfloat16)
        send_back(k, c).start()

    def passed(k, chunks):
        return [functools.partial(pass_back, k, c) for c in chunks]

    def send_far(chunks):
        for c in chunks:
            part, rows = piece(c)
            send_box[REACH, part, rows] = own_parts[part][rows].astype(jnp.bfloat16)

            @pl.when(jnp.logical_not(odd))
            def _(c=c):
                far_pair(c).start()

    when_reached(4, lambda: value_gradients(4), lambda: send_far(first))
    when_reached(3, lambda: value_gradients(3), *passed(3, first))
    when_reached(4, lambda: key_gradients(4), lambda: send_far(second))
    when_reached(3, lambda: key_gradients(3), *passed(3, second))
    when_reached(2, lambda: gradients(2))
    for chunks in (first, second):
        for c in chunks:
            add_pair(c)
        when_reached(2, *passed(2, chunks))
    when_reached(1, lambda: gradients(1))
    when_reached(1, *passed(1, range(CHUNKS)))
    for c in first:
        pass_far(c)
    gradients(0)
    for c in second:
        pass_far(c)
    for h in range(HEADS):
        dq_out[:, h * WIDTH : (h + 1) * WIDTH] = (dq_acc[h] * score_scale).T.astype(jnp.bfloat16)

    @pl.when(has_right)
    def _():
        for c in range(CHUNKS):
            part, rows = piece(c)
            send_back(1, c).wait_recv()
            own_parts[part][rows] += recv_box[0, part, rows].astype(jnp.float32)

    @pl.when(owns_far)
    def _():
        in_use = far_in_use(me)
        for c in range(CHUNKS):
            part, rows = piece(c)

            @pl.when(odd)
            def _(c=c):
                far_on(c).wait_recv()

            own_parts[part][rows] += jnp.where(in_use, far_box[part, rows].astype(jnp.float32), 0.0)

    dv_out[...] = value_part[...].astype(jnp.bfloat16)
    dk_out[...] = (key_part[...] * score_scale).astype(jnp.bfloat16)

    def sent(condition, copy):
        @pl.when(condition)
        def _():
            for c in range(CHUNKS):
                copy(c).wait_send()

    for k in range(REACH - 1):
        sent(has_right & (depth >= k), functools.partial(forward, k))
        sent(depth >= k + 1, functools.partial(send_back, k + 1))
    sent(picks, to_relay)
    sent(is_relay, functools.partial(from_relay, which=0))
    sent(is_relay, functools.partial(from_relay, which=1))
    sent(is_far & jnp.logical_not(odd), far_pair)
    sent(is_far & odd, far_back)
    sent(owns_far & jnp.logical_not(odd), far_on)


def store_kernel(dq, dk, dv, dq_out, dk_out, dv_out, sem):
    copies = [
        pltpu.make_async_copy(dq, dq_out, sem.at[0]),
        pltpu.make_async_copy(dk, dk_out, sem.at[1]),
        pltpu.make_async_copy(dv, dv_out, sem.at[2]),
    ]
    for copy in copies:
        copy.start()
    for copy in copies:
        copy.wait()


def shards(query_rows, key_rows, value_rows, out_grad, doc_lengths):
    bf16, f32 = jnp.bfloat16, jnp.float32
    blocks = REACH + 1
    in_hbm = pl.BlockSpec(memory_space=pltpu.HBM)
    in_vmem = pl.BlockSpec(memory_space=pltpu.VMEM)
    operands = [
        pltpu.with_memory_space_constraint(array, pltpu.HBM)
        for array in (doc_lengths, query_rows, key_rows, value_rows, out_grad)
    ]
    results = tuple(jax.ShapeDtypeStruct(array.shape, bf16) for array in (query_rows, key_rows, value_rows))
    gradients = pl.pallas_call(
        attention_kernel,
        out_shape=results,
        in_specs=[in_hbm] * 5,
        out_specs=(in_vmem, in_vmem, in_vmem),
        scratch_shapes=[
            pltpu.SMEM((DOCS,), jnp.int32),
            pltpu.VMEM((ROWS, HEADS * WIDTH), bf16),
            pltpu.VMEM((ROWS, HEADS * WIDTH), bf16),
            pltpu.VMEM((blocks, ROWS, WIDTH), bf16),
            pltpu.VMEM((blocks, ROWS, WIDTH), bf16),
            pltpu.VMEM((2, ROWS, WIDTH), bf16),
            pltpu.VMEM((2, ROWS, WIDTH), bf16),
            pltpu.VMEM((blocks, WIDTH, ROWS), bf16),
            pltpu.VMEM((blocks, ROWS, ROWS), f32),
            pltpu.VMEM((blocks, HEADS, ROWS, ROWS), f32),
            pltpu.VMEM((blocks, HEADS, ROWS, ROWS), f32),
            pltpu.VMEM((blocks, HEADS, ROWS), f32),
            pltpu.VMEM((blocks, HEADS, ROWS), f32),
            pltpu.VMEM((blocks, HEADS, ROWS), f32),
            pltpu.VMEM((blocks, HEADS, ROWS), f32),
            pltpu.VMEM((HEADS, ROWS), f32),
            pltpu.VMEM((HEADS, WIDTH, ROWS), f32),
            pltpu.VMEM((ROWS, WIDTH), f32),
            pltpu.VMEM((ROWS, WIDTH), f32),
            pltpu.VMEM((blocks, 2, ROWS, WIDTH), bf16),
            pltpu.VMEM((blocks, 2, ROWS, WIDTH), bf16),
            pltpu.VMEM((2, ROWS, WIDTH), bf16),
            pltpu.VMEM((2, ROWS, WIDTH), bf16),
            pltpu.SemaphoreType.DMA((5,)),
            pltpu.SemaphoreType.DMA((blocks, CHUNKS)),
            pltpu.SemaphoreType.DMA((blocks, CHUNKS)),
            pltpu.SemaphoreType.DMA((blocks, CHUNKS)),
            pltpu.SemaphoreType.DMA((blocks, CHUNKS)),
            pltpu.SemaphoreType.DMA((5, CHUNKS)),
            pltpu.SemaphoreType.DMA((5, CHUNKS)),
            pltpu.SemaphoreType.REGULAR,
        ],
        compiler_params=pltpu.CompilerParams(
            collective_id=0, has_side_effects=True, vmem_limit_bytes=48 * 1024 * 1024
        ),
    )(*operands)
    gradients = [pltpu.with_memory_space_constraint(g, pltpu.VMEM) for g in gradients]
    return pl.pallas_call(
        store_kernel,
        out_shape=results,
        in_specs=[in_vmem] * 3,
        out_specs=[in_hbm] * 3,
        scratch_shapes=[pltpu.SemaphoreType.DMA((3,))],
    )(*gradients)


def solution(mesh):
    rows = P(("dp", "ctx"), None)
    return jax.shard_map(
        shards,
        mesh=mesh,
        in_specs=(rows, rows, rows, rows, P("dp")),
        out_specs=(rows, rows, rows),
        check_vma=False,
    )
```

```python
import functools
import math

import jax
import jax.numpy as jnp
from jax import lax
from jax.experimental import pallas as pl
from jax.experimental.pallas import tpu as pltpu
from jax.sharding import PartitionSpec as P

MESH = pl.DeviceIdType.MESH
MASKED = -1e30
HEADS = 8
WIDTH = 128
ROWS = 256
REACH = 4
FIRST = 4
DOCS = 16
PIECES = 2
CHUNKS = 2 * PIECES
SLICE = ROWS // PIECES


def attention_kernel(
    lengths_hbm,
    q_hbm,
    k_hbm,
    v_hbm,
    o_hbm,
    dq_out,
    dk_out,
    dv_out,
    lengths,
    q_ref,
    o_ref,
    keys,
    values,
    picked,
    passing,
    keys_turned,
    bias,
    weights,
    dots,
    tops,
    totals,
    weighted,
    factors,
    deltas,
    dq_acc,
    key_part,
    value_part,
    send_box,
    recv_box,
    far_box,
    pair_box,
    load_sem,
    kv_send_sem,
    kv_recv_sem,
    grad_send_sem,
    grad_recv_sem,
    far_send_sem,
    far_recv_sem,
    far_ready,
):
    me = lax.axis_index("ctx")
    size = 16
    depth = jnp.where(me < FIRST, me, me - FIRST)
    has_left = depth > 0
    has_right = (me != FIRST - 1) & (me != size - 1)
    left = jnp.maximum(me - 1, 0)
    right = jnp.minimum(me + 1, size - 1)

    odd = me % 2 == 1
    picks = odd & (me >= 5) & (me <= 11)
    pick_relay = jnp.where(me == 5, 10, jnp.where(me == 7, 5, jnp.where(me == 9, 15, 0)))
    is_relay = (me == 10) | (me == 5) | (me == 15) | (me == 0)
    relay_to = jnp.where(me == 0, 15, jnp.where(me == 5, 11, jnp.where(me == 10, 9, 13)))
    is_far = me >= 8
    owns_far = (me >= 4) & (me < 12)

    barrier = pltpu.get_barrier_semaphore()

    def greet(condition, device):
        @pl.when(condition)
        def _():
            pl.semaphore_signal(barrier, inc=1, device_id={"ctx": device}, device_id_type=MESH)

    greet(has_left, left)
    greet((me == 10) | (me == 11), 5)
    greet(me == 5, 6)
    greet(me == 8, 10)
    greet(me == 9, 15)
    greet((me == 12) | (me == 13), 14)
    greet(me == 0, 11)
    greet((me == 14) | (me == 15), 0)

    loads = [
        pltpu.make_async_copy(lengths_hbm, lengths, load_sem.at[4]),
        pltpu.make_async_copy(k_hbm, keys.at[0], load_sem.at[0]),
        pltpu.make_async_copy(v_hbm, values.at[0], load_sem.at[1]),
        pltpu.make_async_copy(q_hbm, q_ref, load_sem.at[2]),
        pltpu.make_async_copy(o_hbm, o_ref, load_sem.at[3]),
    ]
    for load in loads:
        load.start()

    expected = has_right.astype(jnp.int32)
    for device, more in ((0, 2), (5, 2), (6, 1), (10, 1), (11, 1), (14, 2), (15, 1)):
        expected += jnp.where(me == device, more, 0)

    @pl.when(me != FIRST - 1)
    def _():
        pl.semaphore_wait(barrier, expected)

    @pl.when(me == 15)
    def _():
        pl.semaphore_signal(far_ready, inc=1, device_id={"ctx": 9}, device_id_type=MESH)

    def remote(source, target, send, recv, device):
        return pltpu.make_async_remote_copy(
            src_ref=source, dst_ref=target, send_sem=send, recv_sem=recv, device_id={"ctx": device}, device_id_type=MESH
        )

    def piece(c):
        return c // PIECES, pl.ds((c % PIECES) * SLICE, SLICE)

    def own_piece(c):
        part, rows = piece(c)
        return (k_hbm, v_hbm)[part].at[rows]

    def forward(k, c):
        part, rows = piece(c)
        place = (keys, values)[part]
        source = own_piece(c) if k == 0 else place.at[k, rows]
        return remote(source, place.at[k + 1, rows], kv_send_sem.at[k, c], kv_recv_sem.at[k + 1, c], right)

    def to_relay(c):
        part, rows = piece(c)
        return remote(
            picked.at[part, rows], passing.at[part, rows], far_send_sem.at[0, c], far_recv_sem.at[0, c], pick_relay
        )

    def from_relay(c, which):
        part, rows = piece(c)
        return remote(
            passing.at[part, rows],
            (keys, values)[part].at[REACH, rows],
            far_send_sem.at[1 + which, c],
            far_recv_sem.at[1, c],
            relay_to - which,
        )

    def send_forward(k, c):
        @pl.when(has_right & (depth >= k))
        def _():
            forward(k, c).start()

    def relay(c, condition):
        @pl.when(is_relay & condition)
        def _():
            to_relay(c).wait_recv()
            for which in (1, 0):
                from_relay(c, which).start()

    for c in range(CHUNKS):
        send_forward(0, c)

    loads[0].wait()
    places = me * ROWS + lax.broadcasted_iota(jnp.int32, (8, ROWS), 1)
    starts = jnp.zeros((8, ROWS), jnp.int32)
    end = jnp.int32(0)
    for d in range(DOCS):
        end = end + lengths[d]
        starts = jnp.where(places >= end, end, starts)
    places, starts = places[:1], starts[:1]
    for k in range(REACH + 1):
        key_places = (me - k) * ROWS + lax.broadcasted_iota(jnp.int32, (ROWS, ROWS), 0)
        allowed = (key_places >= starts) & (key_places <= places)
        bias[k] = jnp.where(allowed, 0.0, MASKED)

    def far_in_use(block):
        start, end = jnp.int32(0), jnp.int32(0)
        for d in range(DOCS):
            end = end + lengths[d]
            start = jnp.where(end <= (block + REACH) * ROWS, end, start)
        return jnp.full((SLICE, WIDTH), start, jnp.int32) < (block + 1) * ROWS

    to_log2 = math.log2(math.e) / math.sqrt(WIDTH)
    score_scale = 1.0 / math.sqrt(WIDTH)
    tops[...] = jnp.full(tops.shape, MASKED, jnp.float32)
    totals[...] = jnp.zeros(totals.shape, jnp.float32)
    weighted[...] = jnp.zeros(weighted.shape, jnp.float32)

    def head(ref, h):
        return ref[:, h * WIDTH : (h + 1) * WIDTH]

    def scores(k):
        block = keys[k]
        for h in range(HEADS):
            raw = lax.dot_general(
                block, head(q_ref, h), (((1,), (1,)), ((), ())), preferred_element_type=jnp.float32
            )
            raw = raw * to_log2 + bias[k]
            top = jnp.max(raw, axis=0, keepdims=True)
            grown = jnp.exp2(raw - top)
            tops[k, h : h + 1, :] = top
            totals[k, h : h + 1, :] = jnp.sum(grown, axis=0, keepdims=True)
            weights[k, h] = grown
        keys_turned[k] = block.T

    def grad_dots(k):
        block = values[k]
        for h in range(HEADS):
            dot = lax.dot_general(
                block, head(o_ref, h), (((1,), (1,)), ((), ())), preferred_element_type=jnp.float32
            )
            dots[k, h] = dot
            weighted[k, h : h + 1, :] = jnp.sum(weights[k, h] * dot, axis=0, keepdims=True)

    def when_reached(k, *steps):
        @pl.when(depth >= k)
        def _():
            for step in steps:
                step()

    def arrive(k, c):
        def step():
            if k == REACH:
                from_relay(c, 0).wait_recv()
            else:
                forward(k - 1, c).wait_recv()
                if k < REACH - 1:
                    send_forward(k, c)

        return step

    def pick(c):
        part, rows = piece(c)
        place = (keys, values)[part]
        before, own = (place[k, rows].astype(jnp.float32) for k in (1, 0))
        picked[part, rows] = jnp.where(far_in_use(me - 1), before, own).astype(jnp.bfloat16)
        if c == 0:

            @pl.when(me == 9)
            def _():
                pl.semaphore_wait(far_ready, 1)

        to_relay(c).start()

    loads[1].wait()
    loads[3].wait()
    scores(0)
    loads[2].wait()
    loads[4].wait()
    grad_dots(0)

    for c in range(CHUNKS):
        when_reached(1, arrive(1, c))

        @pl.when(picks)
        def _(c=c):
            pick(c)

    first, second = range(PIECES), range(PIECES, CHUNKS)
    when_reached(1, lambda: scores(1))
    for c in range(CHUNKS):
        relay(c, me != 10)
        when_reached(2, arrive(2, c))
        relay(c, me == 10)
    when_reached(1, lambda: grad_dots(1))
    when_reached(2, lambda: scores(2))
    when_reached(3, *[arrive(3, c) for c in first], lambda: scores(3))
    when_reached(2, lambda: grad_dots(2))
    when_reached(4, *[arrive(4, c) for c in first], lambda: scores(4))
    when_reached(3, *[arrive(3, c) for c in second], lambda: grad_dots(3))
    when_reached(4, *[arrive(4, c) for c in second], lambda: grad_dots(4))

    top = tops[0]
    for k in range(1, REACH + 1):
        top = jnp.maximum(top, tops[k])
    total = jnp.zeros_like(top)
    weight = jnp.zeros_like(top)
    for k in range(REACH + 1):
        factor = jnp.exp2(tops[k] - top)
        factors[k] = factor
        total = total + factor * totals[k]
        weight = weight + factor * weighted[k]
    inverse = 1.0 / total
    deltas[...] = weight * inverse
    for k in range(REACH + 1):
        factors[k] = factors[k] * inverse
    dq_acc[...] = jnp.zeros(dq_acc.shape, jnp.float32)

    def value_gradients(k):
        value_sum = jnp.zeros((ROWS, WIDTH), jnp.float32)
        for h in range(HEADS):
            soft_low = (weights[k, h] * factors[k, h : h + 1, :]).astype(jnp.bfloat16)
            value_sum = value_sum + jnp.dot(soft_low, head(o_ref, h), preferred_element_type=jnp.float32)
        value_part[...] = value_sum

    def key_gradients(k):
        key_sum = jnp.zeros((ROWS, WIDTH), jnp.float32)
        for h in range(HEADS):
            soft = weights[k, h] * factors[k, h : h + 1, :]
            grad_low = (soft * (dots[k, h] - deltas[h : h + 1, :])).astype(jnp.bfloat16)
            key_sum = key_sum + jnp.dot(grad_low, head(q_ref, h), preferred_element_type=jnp.float32)
            dq_acc[h] += jnp.dot(keys_turned[k], grad_low, preferred_element_type=jnp.float32)
        key_part[...] = key_sum

    def gradients(k):
        value_gradients(k)
        key_gradients(k)

    own_parts = (value_part, key_part)

    def send_back(k, c):
        part, rows = piece(c)
        return remote(
            send_box.at[k, part, rows], recv_box.at[k - 1, part, rows], grad_send_sem.at[k, c], grad_recv_sem.at[k - 1, c], left
        )

    def far_pair(c):
        part, rows = piece(c)
        return remote(
            send_box.at[REACH, part, rows], pair_box.at[part, rows], far_send_sem.at[3, c], far_recv_sem.at[2, c], right
        )

    def far_back(c):
        part, rows = piece(c)
        return remote(
            send_box.at[REACH, part, rows], far_box.at[part, rows], far_send_sem.at[3, c], far_recv_sem.at[3, c], me - 5
        )

    def far_on(c):
        part, rows = piece(c)
        return remote(far_box.at[part, rows], far_box.at[part, rows], far_send_sem.at[4, c], far_recv_sem.at[4, c], right)

    def add_pair(c):
        @pl.when(is_far & odd)
        def _():
            part, rows = piece(c)
            far_pair(c).wait_recv()
            pair = send_box[REACH, part, rows].astype(jnp.float32) + pair_box[part, rows].astype(jnp.float32)
            send_box[REACH, part, rows] = pair.astype(jnp.bfloat16)
            far_back(c).start()

    def pass_far(c):
        @pl.when(owns_far & jnp.logical_not(odd))
        def _():
            far_back(c).wait_recv()
            far_on(c).start()

    def pass_back(k, c):
        part, rows = piece(c)
        own = own_parts[part]
        if k < REACH - 1:

            @pl.when(has_right)
            def _():
                send_back(k + 1, c).wait_recv()
                own[rows] += recv_box[k, part, rows].astype(jnp.float32)

        send_box[k, part, rows] = own[rows].astype(jnp.bfloat16)
        send_back(k, c).start()

    def passed(k, chunks):
        return [functools.partial(pass_back, k, c) for c in chunks]

    def send_far(chunks):
        for c in chunks:
            part, rows = piece(c)
            send_box[REACH, part, rows] = own_parts[part][rows].astype(jnp.bfloat16)

            @pl.when(jnp.logical_not(odd))
            def _(c=c):
                far_pair(c).start()

    when_reached(4, lambda: value_gradients(4), lambda: send_far(first))
    when_reached(3, lambda: value_gradients(3), *passed(3, first))
    when_reached(4, lambda: key_gradients(4), lambda: send_far(second))
    when_reached(3, lambda: key_gradients(3), *passed(3, second))
    when_reached(2, lambda: gradients(2))
    for chunks in (first, second):
        for c in chunks:
            add_pair(c)
        when_reached(2, *passed(2, chunks))
    when_reached(1, lambda: gradients(1))
    when_reached(1, *passed(1, range(CHUNKS)))
    for c in range(CHUNKS):
        pass_far(c)
    gradients(0)
    for h in range(HEADS):
        dq_out[:, h * WIDTH : (h + 1) * WIDTH] = (dq_acc[h] * score_scale).T.astype(jnp.bfloat16)

    @pl.when(has_right)
    def _():
        for c in range(CHUNKS):
            part, rows = piece(c)
            send_back(1, c).wait_recv()
            own_parts[part][rows] += recv_box[0, part, rows].astype(jnp.float32)

    @pl.when(owns_far)
    def _():
        in_use = far_in_use(me)
        for c in range(CHUNKS):
            part, rows = piece(c)

            @pl.when(odd)
            def _(c=c):
                far_on(c).wait_recv()

            own_parts[part][rows] += jnp.where(in_use, far_box[part, rows].astype(jnp.float32), 0.0)

    dv_out[...] = value_part[...].astype(jnp.bfloat16)
    dk_out[...] = (key_part[...] * score_scale).astype(jnp.bfloat16)

    def sent(condition, copy):
        @pl.when(condition)
        def _():
            for c in range(CHUNKS):
                copy(c).wait_send()

    for k in range(REACH - 1):
        sent(has_right & (depth >= k), functools.partial(forward, k))
        sent(depth >= k + 1, functools.partial(send_back, k + 1))
    sent(picks, to_relay)
    sent(is_relay, functools.partial(from_relay, which=0))
    sent(is_relay, functools.partial(from_relay, which=1))
    sent(is_far & jnp.logical_not(odd), far_pair)
    sent(is_far & odd, far_back)
    sent(owns_far & jnp.logical_not(odd), far_on)


def store_kernel(dq, dk, dv, dq_out, dk_out, dv_out, sem):
    copies = [
        pltpu.make_async_copy(dq, dq_out, sem.at[0]),
        pltpu.make_async_copy(dk, dk_out, sem.at[1]),
        pltpu.make_async_copy(dv, dv_out, sem.at[2]),
    ]
    for copy in copies:
        copy.start()
    for copy in copies:
        copy.wait()


def shards(query_rows, key_rows, value_rows, out_grad, doc_lengths):
    bf16, f32 = jnp.bfloat16, jnp.float32
    blocks = REACH + 1
    in_hbm = pl.BlockSpec(memory_space=pltpu.HBM)
    in_vmem = pl.BlockSpec(memory_space=pltpu.VMEM)
    operands = [
        pltpu.with_memory_space_constraint(array, pltpu.HBM)
        for array in (doc_lengths, query_rows, key_rows, value_rows, out_grad)
    ]
    results = tuple(jax.ShapeDtypeStruct(array.shape, bf16) for array in (query_rows, key_rows, value_rows))
    gradients = pl.pallas_call(
        attention_kernel,
        out_shape=results,
        in_specs=[in_hbm] * 5,
        out_specs=(in_vmem, in_vmem, in_vmem),
        scratch_shapes=[
            pltpu.SMEM((DOCS,), jnp.int32),
            pltpu.VMEM((ROWS, HEADS * WIDTH), bf16),
            pltpu.VMEM((ROWS, HEADS * WIDTH), bf16),
            pltpu.VMEM((blocks, ROWS, WIDTH), bf16),
            pltpu.VMEM((blocks, ROWS, WIDTH), bf16),
            pltpu.VMEM((2, ROWS, WIDTH), bf16),
            pltpu.VMEM((2, ROWS, WIDTH), bf16),
            pltpu.VMEM((blocks, WIDTH, ROWS), bf16),
            pltpu.VMEM((blocks, ROWS, ROWS), f32),
            pltpu.VMEM((blocks, HEADS, ROWS, ROWS), f32),
            pltpu.VMEM((blocks, HEADS, ROWS, ROWS), f32),
            pltpu.VMEM((blocks, HEADS, ROWS), f32),
            pltpu.VMEM((blocks, HEADS, ROWS), f32),
            pltpu.VMEM((blocks, HEADS, ROWS), f32),
            pltpu.VMEM((blocks, HEADS, ROWS), f32),
            pltpu.VMEM((HEADS, ROWS), f32),
            pltpu.VMEM((HEADS, WIDTH, ROWS), f32),
            pltpu.VMEM((ROWS, WIDTH), f32),
            pltpu.VMEM((ROWS, WIDTH), f32),
            pltpu.VMEM((blocks, 2, ROWS, WIDTH), bf16),
            pltpu.VMEM((blocks, 2, ROWS, WIDTH), bf16),
            pltpu.VMEM((2, ROWS, WIDTH), bf16),
            pltpu.VMEM((2, ROWS, WIDTH), bf16),
            pltpu.SemaphoreType.DMA((5,)),
            pltpu.SemaphoreType.DMA((blocks, CHUNKS)),
            pltpu.SemaphoreType.DMA((blocks, CHUNKS)),
            pltpu.SemaphoreType.DMA((blocks, CHUNKS)),
            pltpu.SemaphoreType.DMA((blocks, CHUNKS)),
            pltpu.SemaphoreType.DMA((5, CHUNKS)),
            pltpu.SemaphoreType.DMA((5, CHUNKS)),
            pltpu.SemaphoreType.REGULAR,
        ],
        compiler_params=pltpu.CompilerParams(
            collective_id=0, has_side_effects=True, vmem_limit_bytes=48 * 1024 * 1024
        ),
    )(*operands)
    gradients = [pltpu.with_memory_space_constraint(g, pltpu.VMEM) for g in gradients]
    return pl.pallas_call(
        store_kernel,
        out_shape=results,
        in_specs=[in_vmem] * 3,
        out_specs=[in_hbm] * 3,
        scratch_shapes=[pltpu.SemaphoreType.DMA((3,))],
    )(*gradients)


def solution(mesh):
    rows = P(("dp", "ctx"), None)
    return jax.shard_map(
        shards,
        mesh=mesh,
        in_specs=(rows, rows, rows, rows, P("dp")),
        out_specs=(rows, rows, rows),
        check_vma=False,
    )
```

```python
import functools
import math

import jax
import jax.numpy as jnp
from jax import lax
from jax.experimental import pallas as pl
from jax.experimental.pallas import tpu as pltpu
from jax.sharding import PartitionSpec as P

MESH = pl.DeviceIdType.MESH
MASKED = -1e30
HEADS = 8
WIDTH = 128
ROWS = 256
REACH = 4
FIRST = 4
DOCS = 16
PIECES = 2
CHUNKS = 2 * PIECES
SLICE = ROWS // PIECES


def attention_kernel(
    lengths_hbm,
    q_hbm,
    k_hbm,
    v_hbm,
    o_hbm,
    dq_out,
    dk_out,
    dv_out,
    lengths,
    q_ref,
    o_ref,
    keys,
    values,
    picked,
    passing,
    keys_turned,
    bias,
    weights,
    dots,
    tops,
    totals,
    weighted,
    factors,
    deltas,
    dq_acc,
    key_part,
    value_part,
    send_box,
    recv_box,
    far_box,
    pair_box,
    load_sem,
    kv_send_sem,
    kv_recv_sem,
    grad_send_sem,
    grad_recv_sem,
    far_send_sem,
    far_recv_sem,
    far_ready,
):
    me = lax.axis_index("ctx")
    size = 16
    depth = jnp.where(me < FIRST, me, me - FIRST)
    has_left = depth > 0
    has_right = (me != FIRST - 1) & (me != size - 1)
    left = jnp.maximum(me - 1, 0)
    right = jnp.minimum(me + 1, size - 1)

    odd = me % 2 == 1
    picks = odd & (me >= 5) & (me <= 11)
    pick_relay = jnp.where(me == 5, 10, jnp.where(me == 7, 5, jnp.where(me == 9, 15, 0)))
    is_relay = (me == 10) | (me == 5) | (me == 15) | (me == 0)
    relay_to = jnp.where(me == 0, 15, jnp.where(me == 5, 11, jnp.where(me == 10, 9, 13)))
    is_far = me >= 8
    owns_far = (me >= 4) & (me < 12)

    barrier = pltpu.get_barrier_semaphore()

    def greet(condition, device):
        @pl.when(condition)
        def _():
            pl.semaphore_signal(barrier, inc=1, device_id={"ctx": device}, device_id_type=MESH)

    greet(has_left, left)
    greet((me == 10) | (me == 11), 5)
    greet(me == 5, 6)
    greet(me == 8, 10)
    greet(me == 9, 15)
    greet((me == 12) | (me == 13), 14)
    greet(me == 0, 11)
    greet((me == 14) | (me == 15), 0)

    loads = [
        pltpu.make_async_copy(lengths_hbm, lengths, load_sem.at[4]),
        pltpu.make_async_copy(k_hbm, keys.at[0], load_sem.at[0]),
        pltpu.make_async_copy(v_hbm, values.at[0], load_sem.at[1]),
        pltpu.make_async_copy(q_hbm, q_ref, load_sem.at[2]),
        pltpu.make_async_copy(o_hbm, o_ref, load_sem.at[3]),
    ]
    for load in loads:
        load.start()

    expected = has_right.astype(jnp.int32)
    for device, more in ((0, 2), (5, 2), (6, 1), (10, 1), (11, 1), (14, 2), (15, 1)):
        expected += jnp.where(me == device, more, 0)

    @pl.when(me != FIRST - 1)
    def _():
        pl.semaphore_wait(barrier, expected)

    @pl.when(me == 15)
    def _():
        pl.semaphore_signal(far_ready, inc=1, device_id={"ctx": 9}, device_id_type=MESH)

    def remote(source, target, send, recv, device):
        return pltpu.make_async_remote_copy(
            src_ref=source, dst_ref=target, send_sem=send, recv_sem=recv, device_id={"ctx": device}, device_id_type=MESH
        )

    def piece(c):
        return c // PIECES, pl.ds((c % PIECES) * SLICE, SLICE)

    def own_piece(c):
        part, rows = piece(c)
        return (keys, values)[part].at[0, rows]

    def forward(k, c):
        part, rows = piece(c)
        place = (keys, values)[part]
        source = own_piece(c) if k == 0 else place.at[k, rows]
        return remote(source, place.at[k + 1, rows], kv_send_sem.at[k, c], kv_recv_sem.at[k + 1, c], right)

    def to_relay(c):
        part, rows = piece(c)
        return remote(
            picked.at[part, rows], passing.at[part, rows], far_send_sem.at[0, c], far_recv_sem.at[0, c], pick_relay
        )

    def from_relay(c, which):
        part, rows = piece(c)
        return remote(
            passing.at[part, rows],
            (keys, values)[part].at[REACH, rows],
            far_send_sem.at[1 + which, c],
            far_recv_sem.at[1, c],
            relay_to - which,
        )

    def send_forward(k, c):
        @pl.when(has_right & (depth >= k))
        def _():
            forward(k, c).start()

    def relay(c, condition):
        @pl.when(is_relay & condition)
        def _():
            to_relay(c).wait_recv()
            for which in (1, 0):
                from_relay(c, which).start()

    loads[1].wait()
    loads[2].wait()
    for c in range(CHUNKS):
        send_forward(0, c)

    loads[0].wait()
    places = me * ROWS + lax.broadcasted_iota(jnp.int32, (8, ROWS), 1)
    starts = jnp.zeros((8, ROWS), jnp.int32)
    end = jnp.int32(0)
    for d in range(DOCS):
        end = end + lengths[d]
        starts = jnp.where(places >= end, end, starts)
    places, starts = places[:1], starts[:1]
    for k in range(REACH + 1):
        key_places = (me - k) * ROWS + lax.broadcasted_iota(jnp.int32, (ROWS, ROWS), 0)
        allowed = (key_places >= starts) & (key_places <= places)
        bias[k] = jnp.where(allowed, 0.0, MASKED)

    def far_in_use(block):
        start, end = jnp.int32(0), jnp.int32(0)
        for d in range(DOCS):
            end = end + lengths[d]
            start = jnp.where(end <= (block + REACH) * ROWS, end, start)
        return jnp.full((SLICE, WIDTH), start, jnp.int32) < (block + 1) * ROWS

    to_log2 = math.log2(math.e) / math.sqrt(WIDTH)
    score_scale = 1.0 / math.sqrt(WIDTH)
    tops[...] = jnp.full(tops.shape, MASKED, jnp.float32)
    totals[...] = jnp.zeros(totals.shape, jnp.float32)
    weighted[...] = jnp.zeros(weighted.shape, jnp.float32)

    def head(ref, h):
        return ref[:, h * WIDTH : (h + 1) * WIDTH]

    def scores(k):
        block = keys[k]
        for h in range(HEADS):
            raw = lax.dot_general(
                block, head(q_ref, h), (((1,), (1,)), ((), ())), preferred_element_type=jnp.float32
            )
            raw = raw * to_log2 + bias[k]
            top = jnp.max(raw, axis=0, keepdims=True)
            grown = jnp.exp2(raw - top)
            tops[k, h : h + 1, :] = top
            totals[k, h : h + 1, :] = jnp.sum(grown, axis=0, keepdims=True)
            weights[k, h] = grown
        keys_turned[k] = block.T

    def grad_dots(k):
        block = values[k]
        for h in range(HEADS):
            dot = lax.dot_general(
                block, head(o_ref, h), (((1,), (1,)), ((), ())), preferred_element_type=jnp.float32
            )
            dots[k, h] = dot
            weighted[k, h : h + 1, :] = jnp.sum(weights[k, h] * dot, axis=0, keepdims=True)

    def when_reached(k, *steps):
        @pl.when(depth >= k)
        def _():
            for step in steps:
                step()

    def arrive(k, c):
        def step():
            if k == REACH:
                from_relay(c, 0).wait_recv()
            else:
                forward(k - 1, c).wait_recv()
                if k < REACH - 1:
                    send_forward(k, c)

        return step

    def pick(c):
        part, rows = piece(c)
        place = (keys, values)[part]
        before, own = (place[k, rows].astype(jnp.float32) for k in (1, 0))
        picked[part, rows] = jnp.where(far_in_use(me - 1), before, own).astype(jnp.bfloat16)
        if c == 0:

            @pl.when(me == 9)
            def _():
                pl.semaphore_wait(far_ready, 1)

        to_relay(c).start()

    loads[3].wait()
    scores(0)
    loads[4].wait()
    grad_dots(0)

    for c in range(CHUNKS):
        when_reached(1, arrive(1, c))

        @pl.when(picks)
        def _(c=c):
            pick(c)

    first, second = range(PIECES), range(PIECES, CHUNKS)
    when_reached(1, lambda: scores(1))
    for c in range(CHUNKS):
        relay(c, me != 10)
        when_reached(2, arrive(2, c))
        relay(c, me == 10)
    when_reached(1, lambda: grad_dots(1))
    when_reached(2, lambda: scores(2))
    when_reached(3, *[arrive(3, c) for c in first], lambda: scores(3))
    when_reached(2, lambda: grad_dots(2))
    when_reached(4, *[arrive(4, c) for c in first], lambda: scores(4))
    when_reached(3, *[arrive(3, c) for c in second], lambda: grad_dots(3))
    when_reached(4, *[arrive(4, c) for c in second], lambda: grad_dots(4))

    top = tops[0]
    for k in range(1, REACH + 1):
        top = jnp.maximum(top, tops[k])
    total = jnp.zeros_like(top)
    weight = jnp.zeros_like(top)
    for k in range(REACH + 1):
        factor = jnp.exp2(tops[k] - top)
        factors[k] = factor
        total = total + factor * totals[k]
        weight = weight + factor * weighted[k]
    inverse = 1.0 / total
    deltas[...] = weight * inverse
    for k in range(REACH + 1):
        factors[k] = factors[k] * inverse
    dq_acc[...] = jnp.zeros(dq_acc.shape, jnp.float32)

    def value_gradients(k):
        value_sum = jnp.zeros((ROWS, WIDTH), jnp.float32)
        for h in range(HEADS):
            soft_low = (weights[k, h] * factors[k, h : h + 1, :]).astype(jnp.bfloat16)
            value_sum = value_sum + jnp.dot(soft_low, head(o_ref, h), preferred_element_type=jnp.float32)
        value_part[...] = value_sum

    def key_gradients(k):
        key_sum = jnp.zeros((ROWS, WIDTH), jnp.float32)
        for h in range(HEADS):
            soft = weights[k, h] * factors[k, h : h + 1, :]
            grad_low = (soft * (dots[k, h] - deltas[h : h + 1, :])).astype(jnp.bfloat16)
            key_sum = key_sum + jnp.dot(grad_low, head(q_ref, h), preferred_element_type=jnp.float32)
            dq_acc[h] += jnp.dot(keys_turned[k], grad_low, preferred_element_type=jnp.float32)
        key_part[...] = key_sum

    def gradients(k):
        value_gradients(k)
        key_gradients(k)

    own_parts = (value_part, key_part)

    def send_back(k, c):
        part, rows = piece(c)
        return remote(
            send_box.at[k, part, rows], recv_box.at[k - 1, part, rows], grad_send_sem.at[k, c], grad_recv_sem.at[k - 1, c], left
        )

    def far_pair(c):
        part, rows = piece(c)
        return remote(
            send_box.at[REACH, part, rows], pair_box.at[part, rows], far_send_sem.at[3, c], far_recv_sem.at[2, c], right
        )

    def far_back(c):
        part, rows = piece(c)
        return remote(
            send_box.at[REACH, part, rows], far_box.at[part, rows], far_send_sem.at[3, c], far_recv_sem.at[3, c], me - 5
        )

    def far_on(c):
        part, rows = piece(c)
        return remote(far_box.at[part, rows], far_box.at[part, rows], far_send_sem.at[4, c], far_recv_sem.at[4, c], right)

    def add_pair(c):
        @pl.when(is_far & odd)
        def _():
            part, rows = piece(c)
            far_pair(c).wait_recv()
            pair = send_box[REACH, part, rows].astype(jnp.float32) + pair_box[part, rows].astype(jnp.float32)
            send_box[REACH, part, rows] = pair.astype(jnp.bfloat16)
            far_back(c).start()

    def pass_far(c):
        @pl.when(owns_far & jnp.logical_not(odd))
        def _():
            far_back(c).wait_recv()
            far_on(c).start()

    def pass_back(k, c):
        part, rows = piece(c)
        own = own_parts[part]
        if k < REACH - 1:

            @pl.when(has_right)
            def _():
                send_back(k + 1, c).wait_recv()
                own[rows] += recv_box[k, part, rows].astype(jnp.float32)

        send_box[k, part, rows] = own[rows].astype(jnp.bfloat16)
        send_back(k, c).start()

    def passed(k, chunks):
        return [functools.partial(pass_back, k, c) for c in chunks]

    def send_far(chunks):
        for c in chunks:
            part, rows = piece(c)
            send_box[REACH, part, rows] = own_parts[part][rows].astype(jnp.bfloat16)

            @pl.when(jnp.logical_not(odd))
            def _(c=c):
                far_pair(c).start()

    when_reached(4, lambda: value_gradients(4), lambda: send_far(first))
    when_reached(3, lambda: value_gradients(3), *passed(3, first))
    when_reached(4, lambda: key_gradients(4), lambda: send_far(second))
    when_reached(3, lambda: key_gradients(3), *passed(3, second))
    when_reached(2, lambda: gradients(2))
    for chunks in (first, second):
        for c in chunks:
            add_pair(c)
        when_reached(2, *passed(2, chunks))
    when_reached(1, lambda: gradients(1))
    when_reached(1, *passed(1, range(CHUNKS)))
    for c in range(CHUNKS):
        pass_far(c)
    gradients(0)
    for h in range(HEADS):
        dq_out[:, h * WIDTH : (h + 1) * WIDTH] = (dq_acc[h] * score_scale).T.astype(jnp.bfloat16)

    @pl.when(has_right)
    def _():
        for c in range(CHUNKS):
            part, rows = piece(c)
            send_back(1, c).wait_recv()
            own_parts[part][rows] += recv_box[0, part, rows].astype(jnp.float32)

    @pl.when(owns_far)
    def _():
        in_use = far_in_use(me)
        for c in range(CHUNKS):
            part, rows = piece(c)

            @pl.when(odd)
            def _(c=c):
                far_on(c).wait_recv()

            own_parts[part][rows] += jnp.where(in_use, far_box[part, rows].astype(jnp.float32), 0.0)

    dv_out[...] = value_part[...].astype(jnp.bfloat16)
    dk_out[...] = (key_part[...] * score_scale).astype(jnp.bfloat16)

    def sent(condition, copy):
        @pl.when(condition)
        def _():
            for c in range(CHUNKS):
                copy(c).wait_send()

    for k in range(REACH - 1):
        sent(has_right & (depth >= k), functools.partial(forward, k))
        sent(depth >= k + 1, functools.partial(send_back, k + 1))
    sent(picks, to_relay)
    sent(is_relay, functools.partial(from_relay, which=0))
    sent(is_relay, functools.partial(from_relay, which=1))
    sent(is_far & jnp.logical_not(odd), far_pair)
    sent(is_far & odd, far_back)
    sent(owns_far & jnp.logical_not(odd), far_on)


def store_kernel(dq, dk, dv, dq_out, dk_out, dv_out, sem):
    copies = [
        pltpu.make_async_copy(dq, dq_out, sem.at[0]),
        pltpu.make_async_copy(dk, dk_out, sem.at[1]),
        pltpu.make_async_copy(dv, dv_out, sem.at[2]),
    ]
    for copy in copies:
        copy.start()
    for copy in copies:
        copy.wait()


def shards(query_rows, key_rows, value_rows, out_grad, doc_lengths):
    bf16, f32 = jnp.bfloat16, jnp.float32
    blocks = REACH + 1
    in_hbm = pl.BlockSpec(memory_space=pltpu.HBM)
    in_vmem = pl.BlockSpec(memory_space=pltpu.VMEM)
    operands = [
        pltpu.with_memory_space_constraint(array, pltpu.HBM)
        for array in (doc_lengths, query_rows, key_rows, value_rows, out_grad)
    ]
    results = tuple(jax.ShapeDtypeStruct(array.shape, bf16) for array in (query_rows, key_rows, value_rows))
    gradients = pl.pallas_call(
        attention_kernel,
        out_shape=results,
        in_specs=[in_hbm] * 5,
        out_specs=(in_vmem, in_vmem, in_vmem),
        scratch_shapes=[
            pltpu.SMEM((DOCS,), jnp.int32),
            pltpu.VMEM((ROWS, HEADS * WIDTH), bf16),
            pltpu.VMEM((ROWS, HEADS * WIDTH), bf16),
            pltpu.VMEM((blocks, ROWS, WIDTH), bf16),
            pltpu.VMEM((blocks, ROWS, WIDTH), bf16),
            pltpu.VMEM((2, ROWS, WIDTH), bf16),
            pltpu.VMEM((2, ROWS, WIDTH), bf16),
            pltpu.VMEM((blocks, WIDTH, ROWS), bf16),
            pltpu.VMEM((blocks, ROWS, ROWS), f32),
            pltpu.VMEM((blocks, HEADS, ROWS, ROWS), f32),
            pltpu.VMEM((blocks, HEADS, ROWS, ROWS), f32),
            pltpu.VMEM((blocks, HEADS, ROWS), f32),
            pltpu.VMEM((blocks, HEADS, ROWS), f32),
            pltpu.VMEM((blocks, HEADS, ROWS), f32),
            pltpu.VMEM((blocks, HEADS, ROWS), f32),
            pltpu.VMEM((HEADS, ROWS), f32),
            pltpu.VMEM((HEADS, WIDTH, ROWS), f32),
            pltpu.VMEM((ROWS, WIDTH), f32),
            pltpu.VMEM((ROWS, WIDTH), f32),
            pltpu.VMEM((blocks, 2, ROWS, WIDTH), bf16),
            pltpu.VMEM((blocks, 2, ROWS, WIDTH), bf16),
            pltpu.VMEM((2, ROWS, WIDTH), bf16),
            pltpu.VMEM((2, ROWS, WIDTH), bf16),
            pltpu.SemaphoreType.DMA((5,)),
            pltpu.SemaphoreType.DMA((blocks, CHUNKS)),
            pltpu.SemaphoreType.DMA((blocks, CHUNKS)),
            pltpu.SemaphoreType.DMA((blocks, CHUNKS)),
            pltpu.SemaphoreType.DMA((blocks, CHUNKS)),
            pltpu.SemaphoreType.DMA((5, CHUNKS)),
            pltpu.SemaphoreType.DMA((5, CHUNKS)),
            pltpu.SemaphoreType.REGULAR,
        ],
        compiler_params=pltpu.CompilerParams(
            collective_id=0, has_side_effects=True, vmem_limit_bytes=48 * 1024 * 1024
        ),
    )(*operands)
    gradients = [pltpu.with_memory_space_constraint(g, pltpu.VMEM) for g in gradients]
    return pl.pallas_call(
        store_kernel,
        out_shape=results,
        in_specs=[in_vmem] * 3,
        out_specs=[in_hbm] * 3,
        scratch_shapes=[pltpu.SemaphoreType.DMA((3,))],
    )(*gradients)


def solution(mesh):
    rows = P(("dp", "ctx"), None)
    return jax.shard_map(
        shards,
        mesh=mesh,
        in_specs=(rows, rows, rows, rows, P("dp")),
        out_specs=(rows, rows, rows),
        check_vma=False,
    )
```
